128 devices in a mesh: group: 4 (over z_lo, core), cells: 32 (over y, x, z_hi).
Axes of the slice: x: 4, y: 4, z: 4 (z_hi: 2, z_lo: 2; z = z_hi * 2 + z_lo), core: 2. Of those that a mesh axis runs over, the one named last changes fastest.
Arguments:
- state: float32 [4, 3, 90, 131072], P('group', None, None, 'cells'), may hold values from -6 to 6
- vertical_mix: float32 [4, 90, 131072], P('group', None, 'cells'), may hold values from 0.02 to 0.2
- neighbour_weight: float32 [4, 3, 131072], P('group', None, 'cells'), may hold values from 0.02 to 0.15
- neighbours: int32 [4, 3, 131072], P('group', None, 'cells'), may hold values from 0 to 4607, as said below
- land_sea: int32 [131072], P('cells'), may hold values 0 or 1
- remap_weight: float32 [4, 2, 8192, 256], P('group', None, 'cells'), may hold values from 0 to 0.25, as said below
- pair_offsets: int32 [4, 32, 4], P('group', 'cells'), may hold values from 0 to 3840, as said below
- pair_rows: int32 [4, 32, 2], P('group', 'cells'), may hold values from 128 to 256
Outputs:
- new_state: float32 [4, 3, 90, 131072], P('group', None, None, 'cells')
The draws below stay inside these ranges and needn't reach their ends.
Inputs may be any that keep to these rules, and one draw needn't show every extreme that they name: Neighbour positions lie within one rim of the cell; the first two neighbours lie within 4 cells of the cell; both outermost rim cells are used by some cell of every device. `remap_weight`: remap weights are zero where the row and column within a block differ by 4 or more. `pair_offsets`: offsets keep every block inside its device's cells; the ocean rows of strip g's blocks lie in [g * 1365, (g + 1) * 1365).
All inputs are finite; a program needn't handle non-finite values. No bound on the sum of `land_sea` on one device may be relied on, other than what follows from the above.
Results may differ from the reference program's by a relative error of at most 0.0003.
Values sent between devices are 32-bit elements; how exact they have to be, the bound alone decides.
A program may use at most 128 MiB of HBM per device.

```python
import math
import jax
import jax.numpy as jnp
from jax import lax

LEV = 90
NFLD = 3
COLS = 4096
SEGMENTS = 2
BAND = 4
HALO = 256
PR = 256
PC = 256
NC = 131072
N_GROUP = 4
N_CELLS = 32


def draw_neighbours(key, part):
    key = jax.random.fold_in(key, 11)
    near_key, far_key = jax.random.split(key)
    total_cols = N_CELLS * COLS
    near = jax.random.randint(near_key, (N_GROUP, 2, total_cols), -4, 5)
    far = jax.random.randint(far_key, (N_GROUP, 1, total_cols), -HALO, HALO + 1)
    shifts = jnp.concatenate([near, far], 1)
    local = jnp.arange(total_cols, dtype=jnp.int32) % COLS
    places = local[None, None, :] + HALO + shifts
    places = places.at[:, 2, 0::COLS].set(0)
    places = places.at[:, 2, COLS - 1::COLS].set(COLS + 2 * HALO - 1)
    return places.astype(jnp.int32)


def draw_remap_weight(key, part):
    key = jax.random.fold_in(key, 12)
    values = jax.random.uniform(key, (N_GROUP, 2, N_CELLS * PR, PC), jnp.float32, 0.05, 0.25)
    row_place = jnp.arange(N_CELLS * PR, dtype=jnp.int32) % PR
    col_place = jnp.arange(PC, dtype=jnp.int32)
    inside = jnp.abs(row_place[:, None] - col_place[None, :]) < BAND
    return jnp.where(inside[None, None], values, 0.0).astype(jnp.float32)


def draw_pair_offsets(key, part):
    key = jax.random.fold_in(key, 13)
    col_key, row_key = jax.random.split(key)
    strip_cols = COLS // (N_GROUP - 1)
    strip_index = jnp.minimum(jnp.arange(N_GROUP, dtype=jnp.int32), N_GROUP - 2)
    col_starts = jax.random.randint(col_key, (N_GROUP, N_CELLS, 2), 0, COLS - PC + 1)
    row_starts = strip_index[:, None, None] * strip_cols + jax.random.randint(row_key, (N_GROUP, N_CELLS, 2), 0, strip_cols - PR + 1)
    starts = jnp.stack([col_starts[..., 0], row_starts[..., 0], col_starts[..., 1], row_starts[..., 1]], -1)
    starts = starts.at[0, 0, 0].set(COLS - PC)
    starts = starts.at[0, 0, 2].set(COLS - PC)
    starts = starts.at[0, 1, 1].set(0)
    starts = starts.at[0, 1, 0].set(0)
    return starts.astype(jnp.int32)


def draw_pair_rows(key, part):
    key = jax.random.fold_in(key, 14)
    counts = jax.random.randint(key, (N_GROUP, N_CELLS, 2), PR // 2, PR + 1)
    counts = counts.at[0, 0, :].set(PR)
    counts = counts.at[0, 1, :].set(PR // 2)
    return counts.astype(jnp.int32)


def set_ends(values, own_key, low, largest):
    index_at = [jax.random.randint(jax.random.fold_in(own_key, axis), (), 0, length) for axis, length in enumerate(values.shape)]
    longest = values.shape.index(max(values.shape))
    next_to = index_at[:longest] + [(index_at[longest] + 1) % values.shape[longest]] + index_at[longest + 1:]
    return values.at[tuple(index_at)].set(low).at[tuple(next_to)].set(largest)


def block_levels(stream_key, dims, shards, smallest, largest):
    gain, own = 1.0, jax.random.fold_in(stream_key, 6)
    for dim, shards_of in shards:
        heights = jnp.exp(jax.random.uniform(jax.random.fold_in(own, dim), (shards_of,), jnp.float32, smallest / len(shards), largest / len(shards)))
        gain = gain * jnp.repeat(heights, dims[dim] // shards_of).reshape([-1 if axis == dim else 1 for axis in range(len(dims))])
    return gain


def noise(own_key, shape, spread, most, shards=(), kind=jnp.bfloat16):
    gain = block_levels(own_key, shape, shards, -0.22, 0.18) if shards else 1.0
    result = jax.random.normal(own_key, shape, jnp.float32) * spread * gain
    return jnp.minimum(jnp.maximum(result, -most), most).astype(kind)


def setup_inputs(seed: int = 0) -> dict:
    arg_keys = jax.random.split(jax.random.key(seed), 9)
    state = noise(arg_keys[0], (N_GROUP, NFLD, LEV, NC), 1.0, 6.0, ((0, 4), (3, 32)), jnp.float32)
    vertical_mix = jnp.clip(jnp.exp(math.log(0.2) - 2.3025851 * jax.random.uniform(arg_keys[1], (N_GROUP, LEV, NC), jnp.float32) ** block_levels(arg_keys[1], (N_GROUP, LEV, NC), ((0, 4), (2, 32)), -0.2, 0.2)), 0.02, 0.2)
    neighbour_weight = jnp.clip(jnp.exp(math.log(0.15) - 2.014903 * jax.random.uniform(arg_keys[2], (N_GROUP, 3, NC), jnp.float32) ** block_levels(arg_keys[2], (N_GROUP, 3, NC), ((0, 4), (2, 32)), -0.2, 0.2)), 0.02, 0.15)
    neighbours = draw_neighbours(jax.random.fold_in(arg_keys[8], 71), 0)
    land_sea = set_ends((jax.random.randint(arg_keys[4], (NC,), 0, 4) < 3).astype(jnp.int32), jax.random.fold_in(arg_keys[4], 1), 0, 1)
    remap_weight = draw_remap_weight(jax.random.fold_in(arg_keys[8], 71), 0)
    pair_offsets = draw_pair_offsets(jax.random.fold_in(arg_keys[8], 71), 0)
    pair_rows = draw_pair_rows(jax.random.fold_in(arg_keys[8], 71), 0)
    return {"state": state, "vertical_mix": vertical_mix, "neighbour_weight": neighbour_weight, "neighbours": neighbours, "land_sea": land_sea, "remap_weight": remap_weight, "pair_offsets": pair_offsets, "pair_rows": pair_rows}


def pair_coupling(near_air, sea_here, sea_left, weights, offsets, rows, keep):
    pair_height = weights.shape[1]
    pair_width = weights.shape[2]
    columns = near_air.shape[1]
    offsets = offsets.astype(jnp.int32)
    air_gap = jnp.zeros((2, columns), jnp.float32)
    sea_pair = (sea_here, sea_left)
    blocks = []
    for which in range(2):
        col_start = offsets[2 * which]
        row_start = offsets[2 * which + 1]
        live_rows = (jnp.arange(pair_height, dtype=jnp.int32) < rows[which]).astype(jnp.float32)
        block_weight = weights[which] * live_rows[:, None]
        sea_rows = lax.dynamic_slice(sea_pair[which], (jnp.int32(0), row_start), (3, pair_height))
        air_rows = lax.dynamic_slice(near_air, (jnp.int32(0), col_start), (2, pair_width))
        contrib = jnp.dot(sea_rows[:2], block_weight, precision=lax.Precision.HIGHEST)
        contrib = contrib - air_rows * jnp.dot(sea_rows[2:3], block_weight, precision=lax.Precision.HIGHEST)
        window = lax.dynamic_slice(air_gap, (jnp.int32(0), col_start), (2, pair_width))
        air_gap = lax.dynamic_update_slice(air_gap, window + contrib, (jnp.int32(0), col_start))
        blocks.append((block_weight, col_start, row_start))
    air_flux = 0.5 * air_gap * keep
    ocean_terms = []
    for block_weight, col_start, row_start in blocks:
        flux_rows = lax.dynamic_slice(air_flux, (jnp.int32(0), col_start), (2, pair_width))
        ocean_part = jnp.dot(flux_rows, block_weight.T, precision=lax.Precision.HIGHEST)
        ocean_terms.append(lax.dynamic_update_slice(jnp.zeros((2, columns), jnp.float32), ocean_part, (jnp.int32(0), row_start)))
    return air_flux, jnp.stack(ocean_terms)


def vertical_term(fields, mixing):
    upward = (fields[:, 1:] - fields[:, :-1]) * mixing[None, :-1]
    zero_row = jnp.zeros_like(fields[:, :1])
    return jnp.concatenate([upward, zero_row], 1) - jnp.concatenate([zero_row, upward], 1)


def reference(state, vertical_mix, neighbour_weight, neighbours, land_sea, remap_weight, pair_offsets, pair_rows):
    total_cols = N_CELLS * COLS
    groups = N_GROUP
    sea_mask = land_sea.astype(jnp.float32)
    ocean_top = state[groups - 1, :2, 0, :]
    sea_values = jnp.concatenate([ocean_top * sea_mask[None], sea_mask[None]], 0).reshape(3, N_CELLS, COLS)
    sea_left = jnp.roll(sea_values, 1, axis=1)
    coupler = jax.vmap(pair_coupling, in_axes=(1, 1, 1, 0, 0, 0, None))
    ocean_sum = jnp.zeros((N_CELLS, 2, COLS), jnp.float32)
    forcings = []
    for slot in range(groups - 1):
        near_air = state[slot, :2, 0, :].reshape(2, N_CELLS, COLS)
        weights = remap_weight[slot].reshape(2, N_CELLS, PR, PC).transpose(1, 0, 2, 3)
        air_flux, ocean_terms = coupler(near_air, sea_values, sea_left, weights, pair_offsets[slot], pair_rows[slot], jnp.float32(1.0))
        ocean_sum = ocean_sum + ocean_terms[:, 0] + jnp.roll(ocean_terms[:, 1], -1, axis=0)
        forcings.append(air_flux.transpose(1, 0, 2).reshape(2, total_cols))
    ocean_flux = ocean_sum.transpose(1, 0, 2).reshape(2, total_cols)
    forcings.append(-ocean_flux * sea_mask[None])
    block_start = (jnp.arange(total_cols, dtype=jnp.int32) // COLS) * COLS
    outputs = []
    for slot in range(groups):
        fields = state[slot]
        if slot == groups - 1:
            scale = sea_mask[None, None, :]
        else:
            scale = jnp.ones((1, 1, total_cols), jnp.float32)
        places = [(block_start + neighbours[slot, corner] - HALO) % total_cols for corner in range(3)]
        for segment in range(SEGMENTS):
            horizontal = jnp.zeros_like(fields)
            for corner in range(3):
                beside = jnp.take(fields, places[corner], axis=2)
                horizontal = horizontal + neighbour_weight[slot, corner][None, None, :] * (beside - fields)
            fields = fields + (horizontal + vertical_term(fields, vertical_mix[slot])) * scale
        fields = fields.at[:2, 0, :].add(forcings[slot])
        outputs.append(fields)
    return jnp.stack(outputs)
```

```python
import functools

import jax
import jax.numpy as jnp
from jax import lax
from jax.experimental import pallas as pl
from jax.experimental.pallas import tpu as pltpu
from jax.sharding import PartitionSpec as P

LANES = 128
LEV = 90
NFLD = 3
ROWS = 32
TOP = 8
RIM = 2
BATCH = 18
SLAB = 12
SLAB_STEP = 10
STRIPS = 3
MESH = pl.DeviceIdType.MESH


def lane_gather(values, index):
    return jnp.take_along_axis(values, index, axis=1, mode="promise_in_bounds")


def window_pair(rows, shift, lane):
    turned = [pltpu.roll(row, lax.rem(LANES - shift, LANES), 1) for row in rows]
    inside = lane < LANES - shift
    return [jnp.where(inside, turned[i], turned[i + 1]) for i in range(2)]


def placed(parts, first_row, shift, lane, row_of):
    turned = [pltpu.roll(part, shift, 1) for part in parts]
    late = lane >= shift
    zero = jnp.zeros_like(turned[0])
    pieces = [
        jnp.where(late, turned[0], zero),
        jnp.where(late, turned[1], turned[0]),
        jnp.where(late, zero, turned[1]),
    ]
    total = jnp.zeros(row_of.shape, jnp.float32)
    for step, piece in enumerate(pieces):
        total = jnp.where(row_of == first_row + step, piece, total)
    return total


def window_kernel(
    n_cells,
    state,
    mixing_hbm,
    weight,
    place,
    sea_int,
    remap,
    offsets,
    live,
    out,
    first,
    second,
    mixing,
    sea_out,
    sea_in,
    flux,
    near_air,
    term_out,
    term_in,
    load_sem,
    halo_send,
    halo_recv,
    sea_send,
    sea_recv,
    term_send,
    term_recv,
):
    cell = lax.axis_index("cells")
    group = lax.axis_index("group")
    right = lax.rem(cell + 1, n_cells)
    left = lax.rem(cell + n_cells - 1, n_cells)
    is_ocean = group == STRIPS

    def levels_of(field):
        return pl.ds(field * LEV, LEV)

    def load_of(field):
        return pltpu.make_async_copy(
            state.at[levels_of(field)],
            first.at[levels_of(field), pl.ds(TOP, ROWS), :],
            load_sem.at[field],
        )

    mixing_copy = pltpu.make_async_copy(mixing_hbm, mixing, load_sem.at[NFLD])
    for field in range(NFLD):
        load_of(field).start()
    mixing_copy.start()

    barrier = pltpu.get_barrier_semaphore()
    for device in (left, right):
        pl.semaphore_signal(barrier, inc=1, device_id=(group, device), device_id_type=MESH)

    @pl.when(is_ocean)
    def _():
        for strip in range(STRIPS):
            for device in (cell, right):
                pl.semaphore_signal(barrier, inc=1, device_id=(strip, device), device_id_type=MESH)
        pl.semaphore_wait(barrier, 2 + 2 * STRIPS)

    @pl.when(jnp.logical_not(is_ocean))
    def _():
        for device in (cell, left):
            pl.semaphore_signal(barrier, inc=1, device_id=(STRIPS, device), device_id_type=MESH)
        pl.semaphore_wait(barrier, 4)

    def halo(step, field, side):
        levels = levels_of(field)
        if step == 0:
            source, low, high, target = state, 0, ROWS - RIM, first
        else:
            source, low, high, target = second, TOP, TOP + ROWS - RIM, second
        if side == 0:
            begin, land, device = high, TOP - RIM, right
        else:
            begin, land, device = low, TOP + ROWS, left
        return pltpu.make_async_remote_copy(
            src_ref=source.at[levels, pl.ds(begin, RIM), :],
            dst_ref=target.at[levels, pl.ds(land, RIM), :],
            send_sem=halo_send.at[step, side, field],
            recv_sem=halo_recv.at[step, side, field],
            device_id=(group, device),
            device_id_type=MESH,
        )

    for field in range(NFLD):
        for side in range(2):
            halo(0, field, side).start()

    def sea_copy(strip, pair):
        return pltpu.make_async_remote_copy(
            src_ref=sea_out.at[:, pl.ds(strip * SLAB_STEP, SLAB), :],
            dst_ref=sea_in.at[pair, :, pl.ds(0, SLAB), :],
            send_sem=sea_send.at[strip, pair],
            recv_sem=sea_recv.at[pair],
            device_id=(strip, (cell, right)[pair]),
            device_id_type=MESH,
        )

    def term_copy(strip, pair):
        return pltpu.make_async_remote_copy(
            src_ref=term_out.at[pair],
            dst_ref=term_in.at[strip, pair],
            send_sem=term_send.at[pair],
            recv_sem=term_recv.at[strip, pair],
            device_id=(STRIPS, (cell, left)[pair]),
            device_id_type=MESH,
        )

    sea_mask = sea_int[...].astype(jnp.float32)
    for field in range(NFLD):
        load_of(field).wait()
    mixing_copy.wait()

    @pl.when(is_ocean)
    def _():
        for field in range(2):
            sea_out[field] = first[field * LEV, TOP : TOP + ROWS, :] * sea_mask
        sea_out[2] = sea_mask
        for strip in range(STRIPS):
            for pair in range(2):
                sea_copy(strip, pair).start()

    lane8 = lax.broadcasted_iota(jnp.int32, (8, LANES), 1)
    row8 = lax.broadcasted_iota(jnp.int32, (8, LANES), 0)
    half = lane8 < LANES // 2

    def advance(source, target, target_top, field, chunk):
        rows = slice(chunk * 8, chunk * 8 + 8)
        position = [place[k, rows, :] for k in range(3)]
        index = [p & (LANES - 1) for p in position]
        apart = [(p >> 7) - (row8 + (chunk * 8 + RIM)) for p in position]
        part = [weight[k, rows, :] for k in range(3)]
        centre = part[0] + part[1] + part[2]
        scale = jnp.where(is_ocean, sea_int[rows, :].astype(jnp.float32), 1.0)
        far_at = [apart[2] == g for g in (-2, -1, 1, 2)]
        here = [apart[k] == 0 for k in range(2)]
        base = TOP + chunk * 8
        steps = LEV // BATCH

        def batch(t, carry):
            begin, below = carry
            level = t * BATCH
            at = field * LEV + level
            x = [begin] + [source[at + b, pl.ds(base, 8), :] for b in range(1, BATCH + 1)]
            before = [source[at + b, pl.ds(base - 1, 8), :] for b in range(BATCH)]
            after = [source[at + b, pl.ds(base + 1, 8), :] for b in range(BATCH)]
            mixed = []
            for b in range(BATCH):
                before2 = source[at + b, pl.ds(base - 2, 8), :]
                after2 = source[at + b, pl.ds(base + 2, 8), :]
                value = lane_gather(x[b], index[2])
                for chosen, row in zip(far_at, (before2, before[b], after[b], after2)):
                    value = jnp.where(chosen, lane_gather(row, index[2]), value)
                mixed.append(part[2] * value - centre * x[b])
            edge = [jnp.where(half, after[b], before[b]) for b in range(BATCH)]
            for k in range(2):
                for b in range(BATCH):
                    value = jnp.where(here[k], lane_gather(x[b], index[k]), lane_gather(edge[b], index[k]))
                    mixed[b] = mixed[b] + part[k] * value
            for b in range(BATCH):
                upward = mixing[level + b, rows, :] * (x[b + 1] - x[b])
                if b == BATCH - 1:
                    upward = jnp.where(t == steps - 1, 0.0, upward)
                target[at + b, target_top + chunk * 8 : target_top + chunk * 8 + 8, :] = x[b] + scale * (
                    mixed[b] + (upward - below)
                )
                below = upward
            return x[BATCH], below

        start = source[field * LEV, pl.ds(base, 8), :]
        lax.fori_loop(0, steps, batch, (start, jnp.zeros((8, LANES), jnp.float32)))

    def each_field(body):
        lax.fori_loop(0, NFLD, lambda field, c: (body(field), c)[1], 0)

    def inner_first(field):
        for chunk in (1, 2):
            advance(first, second, TOP, field, chunk)

    each_field(inner_first)

    lane1 = lax.broadcasted_iota(jnp.int32, (1, LANES), 1)
    lane3 = lax.broadcasted_iota(jnp.int32, (3, LANES), 1)
    lane2 = lax.broadcasted_iota(jnp.int32, (2, LANES), 1)
    row_of = lax.broadcasted_iota(jnp.int32, (ROWS, LANES), 0)
    slab_row = lax.broadcasted_iota(jnp.int32, (16, LANES), 0)

    @pl.when(jnp.logical_not(is_ocean))
    def _():
        gap = [jnp.zeros((ROWS, LANES), jnp.float32) for _ in range(2)]
        for field in range(2):
            near_air[field, 0:ROWS, :] = first[field * LEV, TOP : TOP + ROWS, :]
            near_air[field, ROWS:, :] = jnp.zeros((8, LANES), jnp.float32)
        for pair in range(2):
            sea_copy(0, pair).wait_recv()
        for pair in range(2):
            col = offsets[2 * pair]
            row = offsets[2 * pair + 1] - group * (SLAB_STEP * LANES)
            rows_live = live[pair]
            sea = window_pair(
                [sea_in[pair, :, jnp.clip((row >> 7) + i, 0, 15), :] for i in range(3)],
                row & (LANES - 1),
                lane3,
            )
            sea = [jnp.where(lane3 + i * LANES < rows_live, sea[i], 0.0) for i in range(2)]
            moved = jnp.zeros((3, 2 * LANES), jnp.float32)
            for i in range(2):
                moved = moved + jnp.dot(
                    sea[i],
                    remap[pair, i * LANES : (i + 1) * LANES, :],
                    precision=lax.Precision.HIGHEST,
                    preferred_element_type=jnp.float32,
                )
            for field in range(2):
                air = window_pair(
                    [near_air[field, pl.ds(jnp.clip((col >> 7) + i, 0, ROWS), 1), :] for i in range(3)],
                    col & (LANES - 1),
                    lane1,
                )
                parts = [
                    moved[field : field + 1, i * LANES : (i + 1) * LANES]
                    - air[i] * moved[2:3, i * LANES : (i + 1) * LANES]
                    for i in range(2)
                ]
                gap[field] = gap[field] + placed(parts, col >> 7, col & (LANES - 1), lane1, row_of)
        for field in range(2):
            flux[field, 0:ROWS, :] = 0.5 * gap[field]
            flux[field, ROWS:, :] = jnp.zeros((8, LANES), jnp.float32)
        for pair in range(2):
            col = offsets[2 * pair]
            row = offsets[2 * pair + 1] - group * (SLAB_STEP * LANES)
            rows_live = live[pair]
            back = window_pair(
                [flux[:, jnp.clip((col >> 7) + i, 0, ROWS), :] for i in range(3)], col & (LANES - 1), lane2
            )
            parts = []
            for i in range(2):
                block = remap[pair, i * LANES : (i + 1) * LANES, :]
                term = jnp.zeros((2, LANES), jnp.float32)
                for j in range(2):
                    term = term + lax.dot_general(
                        back[j],
                        block[:, j * LANES : (j + 1) * LANES],
                        (((1,), (1,)), ((), ())),
                        precision=lax.Precision.HIGHEST,
                        preferred_element_type=jnp.float32,
                    )
                parts.append(jnp.where(lane2 + i * LANES < rows_live, term, 0.0))
            for field in range(2):
                laid = placed(
                    [part[field : field + 1] for part in parts], row >> 7, row & (LANES - 1), lane1, slab_row
                )
                term_out[pair, field] = laid
        for strip in range(STRIPS):

            @pl.when(group == strip)
            def _():
                for pair in range(2):
                    term_copy(strip, pair).start()

    def outer_first(field):
        for side, chunk in ((0, 0), (1, ROWS // 8 - 1)):
            halo(0, field, side).wait_recv()
            advance(first, second, TOP, field, chunk)
            halo(1, field, 1 - side).start()

    each_field(outer_first)

    def inner_second(field):
        for chunk in (1, 2):
            advance(second, out, 0, field, chunk)

    each_field(inner_second)

    @pl.when(is_ocean)
    def _():
        for field in range(2):
            flux[field] = jnp.zeros((ROWS + 8, LANES), jnp.float32)
        for strip in range(STRIPS):
            for pair in range(2):
                term_copy(strip, pair).wait_recv()
                for field in range(2):
                    at = slice(strip * SLAB_STEP, strip * SLAB_STEP + SLAB)
                    flux[field, at, :] = flux[field, at, :] + term_in[strip, pair, field, 0:SLAB, :]
        for field in range(2):
            flux[field, 0:ROWS, :] = -flux[field, 0:ROWS, :] * sea_mask

    def outer_second(field):
        for side, chunk in ((0, 0), (1, ROWS // 8 - 1)):
            halo(1, field, side).wait_recv()
            advance(second, out, 0, field, chunk)

    each_field(outer_second)
    for field in range(2):
        out[field * LEV] = out[field * LEV] + flux[field, 0:ROWS, :]

    for step in range(2):
        for field in range(NFLD):
            for side in range(2):
                halo(step, field, side).wait_send()

    @pl.when(is_ocean)
    def _():
        for strip in range(STRIPS):
            for pair in range(2):
                sea_copy(strip, pair).wait_send()

    @pl.when(jnp.logical_not(is_ocean))
    def _():
        for pair in range(2):
            term_copy(0, pair).wait_send()


def per_device(
    n_cells,
    state,
    vertical_mix,
    neighbour_weight,
    neighbours,
    land_sea,
    remap_weight,
    pair_offsets,
    pair_rows,
):
    any_space = pl.BlockSpec(memory_space=pl.ANY)
    vmem = pl.BlockSpec(memory_space=pltpu.VMEM)
    smem = pl.BlockSpec(memory_space=pltpu.SMEM)
    levels = NFLD * LEV
    f32 = jnp.float32
    dma = pltpu.SemaphoreType.DMA
    out = pl.pallas_call(
        functools.partial(window_kernel, n_cells),
        out_shape=jax.ShapeDtypeStruct((levels, ROWS, LANES), f32),
        in_specs=[any_space, any_space, vmem, vmem, vmem, vmem, smem, smem],
        out_specs=vmem,
        scratch_shapes=[
            pltpu.VMEM((levels + 2, 48, LANES), f32),
            pltpu.VMEM((levels + 2, 48, LANES), f32),
            pltpu.VMEM((LEV, ROWS, LANES), f32),
            pltpu.VMEM((3, ROWS, LANES), f32),
            pltpu.VMEM((2, 3, 16, LANES), f32),
            pltpu.VMEM((2, ROWS + 8, LANES), f32),
            pltpu.VMEM((2, ROWS + 8, LANES), f32),
            pltpu.VMEM((2, 2, 16, LANES), f32),
            pltpu.VMEM((STRIPS, 2, 2, 16, LANES), f32),
            dma((NFLD + 1,)),
            dma((2, 2, NFLD)),
            dma((2, 2, NFLD)),
            dma((STRIPS, 2)),
            dma((2,)),
            dma((2,)),
            dma((STRIPS, 2)),
        ],
        compiler_params=pltpu.CompilerParams(
            collective_id=0, has_side_effects=True, vmem_limit_bytes=48 * 1024 * 1024
        ),
        name="window",
    )(
        state.reshape(levels, ROWS, LANES),
        vertical_mix.reshape(LEV, ROWS, LANES),
        neighbour_weight.reshape(3, ROWS, LANES),
        neighbours.reshape(3, ROWS, LANES),
        land_sea.reshape(ROWS, LANES),
        remap_weight[0],
        pair_offsets.reshape(4),
        pair_rows.reshape(2),
    )
    return out.reshape(1, NFLD, LEV, ROWS * LANES)


def solution(mesh):
    return jax.shard_map(
        functools.partial(per_device, mesh.shape["cells"]),
        mesh=mesh,
        in_specs=(
            P("group", None, None, "cells"),
            P("group", None, "cells"),
            P("group", None, "cells"),
            P("group", None, "cells"),
            P("cells"),
            P("group", None, "cells", None),
            P("group", "cells", None),
            P("group", "cells", None),
        ),
        out_specs=P("group", None, None, "cells"),
        check_vma=False,
    )
```

```python
import functools

import jax
import jax.numpy as jnp
from jax import lax
from jax.experimental import pallas as pl
from jax.experimental.pallas import tpu as pltpu
from jax.sharding import PartitionSpec as P

LANES = 128
LEV = 90
NFLD = 3
ROWS = 32
TOP = 8
RIM = 2
BATCH = 30
SLAB = 12
SLAB_STEP = 10
STRIPS = 3
MESH = pl.DeviceIdType.MESH


def lane_gather(values, index):
    return jnp.take_along_axis(values, index, axis=1, mode="promise_in_bounds")


def window_pair(rows, shift, lane):
    turned = [pltpu.roll(row, lax.rem(LANES - shift, LANES), 1) for row in rows]
    inside = lane < LANES - shift
    return [jnp.where(inside, turned[i], turned[i + 1]) for i in range(2)]


def placed(parts, first_row, shift, lane, row_of):
    turned = [pltpu.roll(part, shift, 1) for part in parts]
    late = lane >= shift
    zero = jnp.zeros_like(turned[0])
    pieces = [
        jnp.where(late, turned[0], zero),
        jnp.where(late, turned[1], turned[0]),
        jnp.where(late, zero, turned[1]),
    ]
    total = jnp.zeros(row_of.shape, jnp.float32)
    for step, piece in enumerate(pieces):
        total = jnp.where(row_of == first_row + step, piece, total)
    return total


def window_kernel(
    n_cells,
    state,
    mixing_hbm,
    weight_hbm,
    place_hbm,
    sea_hbm,
    remap_hbm,
    offsets_hbm,
    live_hbm,
    out,
    flux,
    weight,
    place,
    sea_int,
    remap,
    offsets,
    live,
    first,
    second,
    mixing,
    sea_out,
    sea_in,
    near_air,
    term_out,
    term_in,
    load_sem,
    halo_send,
    halo_recv,
    sea_send,
    sea_recv,
    term_send,
    term_recv,
):
    cell = lax.axis_index("cells")
    group = lax.axis_index("group")
    right = lax.rem(cell + 1, n_cells)
    left = lax.rem(cell + n_cells - 1, n_cells)
    is_ocean = group == STRIPS

    def levels_of(field):
        return pl.ds(field * LEV, LEV)

    def load_of(field):
        return pltpu.make_async_copy(
            state.at[levels_of(field)],
            first.at[levels_of(field), pl.ds(TOP, ROWS), :],
            load_sem.at[field],
        )

    surface = (sea_hbm, sea_int), (place_hbm, place), (weight_hbm, weight), (mixing_hbm, mixing)
    coupling = (remap_hbm, remap), (offsets_hbm, offsets), (live_hbm, live)
    others = [
        pltpu.make_async_copy(source, target, load_sem.at[NFLD + i])
        for i, (source, target) in enumerate(surface + coupling)
    ]
    for field in range(NFLD):
        load_of(field).start()
    for copy in others:
        copy.start()

    barrier = pltpu.get_barrier_semaphore()
    for device in (left, right):
        pl.semaphore_signal(barrier, inc=1, device_id=(group, device), device_id_type=MESH)

    @pl.when(is_ocean)
    def _():
        for strip in range(STRIPS):
            for device in (cell, right):
                pl.semaphore_signal(barrier, inc=1, device_id=(strip, device), device_id_type=MESH)
        pl.semaphore_wait(barrier, 2 + 2 * STRIPS)

    @pl.when(jnp.logical_not(is_ocean))
    def _():
        for device in (cell, left):
            pl.semaphore_signal(barrier, inc=1, device_id=(STRIPS, device), device_id_type=MESH)
        pl.semaphore_wait(barrier, 4)

    def halo(step, field, side):
        levels = levels_of(field)
        if step == 0:
            source, low, high, target = state, 0, ROWS - RIM, first
        else:
            source, low, high, target = second, TOP, TOP + ROWS - RIM, second
        if side == 0:
            begin, land, device = high, TOP - RIM, right
        else:
            begin, land, device = low, TOP + ROWS, left
        return pltpu.make_async_remote_copy(
            src_ref=source.at[levels, pl.ds(begin, RIM), :],
            dst_ref=target.at[levels, pl.ds(land, RIM), :],
            send_sem=halo_send.at[step, side, field],
            recv_sem=halo_recv.at[step, side, field],
            device_id=(group, device),
            device_id_type=MESH,
        )

    for field in range(NFLD):
        for side in range(2):
            halo(0, field, side).start()

    def sea_copy(strip, pair):
        return pltpu.make_async_remote_copy(
            src_ref=sea_out.at[:, pl.ds(strip * SLAB_STEP, SLAB), :],
            dst_ref=sea_in.at[pair, :, pl.ds(0, SLAB), :],
            send_sem=sea_send.at[strip, pair],
            recv_sem=sea_recv.at[pair],
            device_id=(strip, (cell, right)[pair]),
            device_id_type=MESH,
        )

    def term_copy(strip, pair):
        return pltpu.make_async_remote_copy(
            src_ref=term_out.at[pair],
            dst_ref=term_in.at[strip, pair],
            send_sem=term_send.at[pair],
            recv_sem=term_recv.at[strip, pair],
            device_id=(STRIPS, (cell, left)[pair]),
            device_id_type=MESH,
        )

    for field in range(NFLD):
        load_of(field).wait()
    for copy in others:
        copy.wait()
    sea_mask = sea_int[...].astype(jnp.float32)

    @pl.when(is_ocean)
    def _():
        for field in range(2):
            sea_out[field] = first[field * LEV, TOP : TOP + ROWS, :] * sea_mask
        sea_out[2] = sea_mask
        for strip in range(STRIPS):
            for pair in range(2):
                sea_copy(strip, pair).start()

    lane8 = lax.broadcasted_iota(jnp.int32, (8, LANES), 1)
    row8 = lax.broadcasted_iota(jnp.int32, (8, LANES), 0)
    half = lane8 < LANES // 2

    def advance(source, target, target_top, field, chunk):
        rows = slice(chunk * 8, chunk * 8 + 8)
        position = [place[k, rows, :] for k in range(3)]
        index = [p & (LANES - 1) for p in position]
        apart = [(p >> 7) - (row8 + (chunk * 8 + RIM)) for p in position]
        part = [weight[k, rows, :] for k in range(3)]
        centre = part[0] + part[1] + part[2]
        scale = jnp.where(is_ocean, sea_int[rows, :].astype(jnp.float32), 1.0)
        far_at = [apart[2] == g for g in (-2, -1, 1, 2)]
        here = [apart[k] == 0 for k in range(2)]
        base = TOP + chunk * 8
        steps = LEV // BATCH

        def batch(t, carry):
            begin, below = carry
            level = t * BATCH
            at = field * LEV + level
            x = [begin] + [source[at + b, pl.ds(base, 8), :] for b in range(1, BATCH + 1)]
            before = [source[at + b, pl.ds(base - 1, 8), :] for b in range(BATCH)]
            after = [source[at + b, pl.ds(base + 1, 8), :] for b in range(BATCH)]
            mixed = []
            for b in range(BATCH):
                before2 = source[at + b, pl.ds(base - 2, 8), :]
                after2 = source[at + b, pl.ds(base + 2, 8), :]
                value = lane_gather(x[b], index[2])
                for chosen, row in zip(far_at, (before2, before[b], after[b], after2)):
                    value = jnp.where(chosen, lane_gather(row, index[2]), value)
                mixed.append(part[2] * value - centre * x[b])
            edge = [jnp.where(half, after[b], before[b]) for b in range(BATCH)]
            for k in range(2):
                for b in range(BATCH):
                    value = jnp.where(here[k], lane_gather(x[b], index[k]), lane_gather(edge[b], index[k]))
                    mixed[b] = mixed[b] + part[k] * value
            for b in range(BATCH):
                upward = mixing[level + b, rows, :] * (x[b + 1] - x[b])
                if b == BATCH - 1:
                    upward = jnp.where(t == steps - 1, 0.0, upward)
                target[at + b, target_top + chunk * 8 : target_top + chunk * 8 + 8, :] = x[b] + scale * (
                    mixed[b] + (upward - below)
                )
                below = upward
            return x[BATCH], below

        start = source[field * LEV, pl.ds(base, 8), :]
        lax.fori_loop(0, steps, batch, (start, jnp.zeros((8, LANES), jnp.float32)))

    def each_field(body):
        lax.fori_loop(0, NFLD, lambda field, c: (body(field), c)[1], 0)

    def inner_first(field):
        for chunk in (1, 2):
            advance(first, second, TOP, field, chunk)

    each_field(inner_first)

    lane1 = lax.broadcasted_iota(jnp.int32, (1, LANES), 1)
    lane3 = lax.broadcasted_iota(jnp.int32, (3, LANES), 1)
    lane2 = lax.broadcasted_iota(jnp.int32, (2, LANES), 1)
    row_of = lax.broadcasted_iota(jnp.int32, (ROWS, LANES), 0)
    slab_row = lax.broadcasted_iota(jnp.int32, (16, LANES), 0)

    @pl.when(jnp.logical_not(is_ocean))
    def _():
        gap = [jnp.zeros((ROWS, LANES), jnp.float32) for _ in range(2)]
        for field in range(2):
            near_air[field, 0:ROWS, :] = first[field * LEV, TOP : TOP + ROWS, :]
            near_air[field, ROWS:, :] = jnp.zeros((8, LANES), jnp.float32)
        for pair in range(2):
            sea_copy(0, pair).wait_recv()
        for pair in range(2):
            col = offsets[2 * pair]
            row = offsets[2 * pair + 1] - group * (SLAB_STEP * LANES)
            rows_live = live[pair]
            sea = window_pair(
                [sea_in[pair, :, jnp.clip((row >> 7) + i, 0, 15), :] for i in range(3)],
                row & (LANES - 1),
                lane3,
            )
            sea = [jnp.where(lane3 + i * LANES < rows_live, sea[i], 0.0) for i in range(2)]
            moved = jnp.zeros((3, 2 * LANES), jnp.float32)
            for i in range(2):
                moved = moved + jnp.dot(
                    sea[i],
                    remap[pair, i * LANES : (i + 1) * LANES, :],
                    precision=lax.Precision.HIGHEST,
                    preferred_element_type=jnp.float32,
                )
            for field in range(2):
                air = window_pair(
                    [near_air[field, pl.ds(jnp.clip((col >> 7) + i, 0, ROWS), 1), :] for i in range(3)],
                    col & (LANES - 1),
                    lane1,
                )
                parts = [
                    moved[field : field + 1, i * LANES : (i + 1) * LANES]
                    - air[i] * moved[2:3, i * LANES : (i + 1) * LANES]
                    for i in range(2)
                ]
                gap[field] = gap[field] + placed(parts, col >> 7, col & (LANES - 1), lane1, row_of)
        for field in range(2):
            flux[field, 0:ROWS, :] = 0.5 * gap[field]
            flux[field, ROWS:, :] = jnp.zeros((8, LANES), jnp.float32)
        for pair in range(2):
            col = offsets[2 * pair]
            row = offsets[2 * pair + 1] - group * (SLAB_STEP * LANES)
            rows_live = live[pair]
            back = window_pair(
                [flux[:, jnp.clip((col >> 7) + i, 0, ROWS), :] for i in range(3)], col & (LANES - 1), lane2
            )
            parts = []
            for i in range(2):
                block = remap[pair, i * LANES : (i + 1) * LANES, :]
                term = jnp.zeros((2, LANES), jnp.float32)
                for j in range(2):
                    term = term + lax.dot_general(
                        back[j],
                        block[:, j * LANES : (j + 1) * LANES],
                        (((1,), (1,)), ((), ())),
                        precision=lax.Precision.HIGHEST,
                        preferred_element_type=jnp.float32,
                    )
                parts.append(jnp.where(lane2 + i * LANES < rows_live, term, 0.0))
            for field in range(2):
                laid = placed(
                    [part[field : field + 1] for part in parts], row >> 7, row & (LANES - 1), lane1, slab_row
                )
                term_out[pair, field] = laid
        for strip in range(STRIPS):

            @pl.when(group == strip)
            def _():
                for pair in range(2):
                    term_copy(strip, pair).start()

    def outer_first(field):
        for side, chunk in ((0, 0), (1, ROWS // 8 - 1)):
            halo(0, field, side).wait_recv()
            advance(first, second, TOP, field, chunk)
            halo(1, field, 1 - side).start()

    each_field(outer_first)

    def inner_second(field):
        for chunk in (1, 2):
            advance(second, out, 0, field, chunk)

    each_field(inner_second)

    @pl.when(is_ocean)
    def _():
        for field in range(2):
            flux[field] = jnp.zeros((ROWS + 8, LANES), jnp.float32)
        for strip in range(STRIPS):
            for pair in range(2):
                term_copy(strip, pair).wait_recv()
                for field in range(2):
                    at = slice(strip * SLAB_STEP, strip * SLAB_STEP + SLAB)
                    flux[field, at, :] = flux[field, at, :] + term_in[strip, pair, field, 0:SLAB, :]
        for field in range(2):
            flux[field, 0:ROWS, :] = -flux[field, 0:ROWS, :] * sea_mask

    def outer_second(field):
        for side, chunk in ((0, 0), (1, ROWS // 8 - 1)):
            halo(1, field, side).wait_recv()
            advance(second, out, 0, field, chunk)

    each_field(outer_second)

    for step in range(2):
        for field in range(NFLD):
            for side in range(2):
                halo(step, field, side).wait_send()

    @pl.when(is_ocean)
    def _():
        for strip in range(STRIPS):
            for pair in range(2):
                sea_copy(strip, pair).wait_send()

    @pl.when(jnp.logical_not(is_ocean))
    def _():
        for pair in range(2):
            term_copy(0, pair).wait_send()


def store_kernel(fields, forcing, out, top, sem):
    copies = []
    for field in range(NFLD):
        first = field * LEV + (1 if field < 2 else 0)
        rows = pl.ds(first, (field + 1) * LEV - first)
        copies.append(pltpu.make_async_copy(fields.at[rows], out.at[rows], sem.at[field]))
    for copy in copies:
        copy.start()
    for field in range(2):
        top[field] = fields[field * LEV] + forcing[field, 0:ROWS, :]
        copy = pltpu.make_async_copy(top.at[field], out.at[field * LEV], sem.at[NFLD + field])
        copy.start()
        copies.append(copy)
    for copy in copies:
        copy.wait()


def per_device(
    n_cells,
    state,
    vertical_mix,
    neighbour_weight,
    neighbours,
    land_sea,
    remap_weight,
    pair_offsets,
    pair_rows,
):
    hbm = pl.BlockSpec(memory_space=pltpu.HBM)
    vmem = pl.BlockSpec(memory_space=pltpu.VMEM)
    levels = NFLD * LEV
    f32 = jnp.float32
    dma = pltpu.SemaphoreType.DMA
    operands = (
        state.reshape(levels, ROWS, LANES),
        vertical_mix.reshape(LEV, ROWS, LANES),
        neighbour_weight.reshape(3, ROWS, LANES),
        neighbours.reshape(3, ROWS, LANES),
        land_sea.reshape(ROWS, LANES),
        remap_weight[0],
        pair_offsets.reshape(4),
        pair_rows.reshape(2),
    )
    fields, forcing = pl.pallas_call(
        functools.partial(window_kernel, n_cells),
        out_shape=(pltpu.VMEM((levels, ROWS, LANES), f32), pltpu.VMEM((2, ROWS + 8, LANES), f32)),
        in_specs=[hbm] * 8,
        out_specs=(vmem, vmem),
        scratch_shapes=[
            pltpu.VMEM((3, ROWS, LANES), f32),
            pltpu.VMEM((3, ROWS, LANES), jnp.int32),
            pltpu.VMEM((ROWS, LANES), jnp.int32),
            pltpu.VMEM((2, 2 * LANES, 2 * LANES), f32),
            pltpu.SMEM((4,), jnp.int32),
            pltpu.SMEM((2,), jnp.int32),
            pltpu.VMEM((levels + 2, 48, LANES), f32),
            pltpu.VMEM((levels + 2, 48, LANES), f32),
            pltpu.VMEM((LEV, ROWS, LANES), f32),
            pltpu.VMEM((3, ROWS, LANES), f32),
            pltpu.VMEM((2, 3, 16, LANES), f32),
            pltpu.VMEM((2, ROWS + 8, LANES), f32),
            pltpu.VMEM((2, 2, 16, LANES), f32),
            pltpu.VMEM((STRIPS, 2, 2, 16, LANES), f32),
            dma((NFLD + 7,)),
            dma((2, 2, NFLD)),
            dma((2, 2, NFLD)),
            dma((STRIPS, 2)),
            dma((2,)),
            dma((2,)),
            dma((STRIPS, 2)),
        ],
        compiler_params=pltpu.CompilerParams(
            collective_id=0, has_side_effects=True, vmem_limit_bytes=40 * 1024 * 1024
        ),
        name="window",
    )(*(pltpu.with_memory_space_constraint(operand, pltpu.HBM) for operand in operands))
    out = pl.pallas_call(
        store_kernel,
        out_shape=jax.ShapeDtypeStruct((levels, ROWS, LANES), f32),
        in_specs=[vmem, vmem],
        out_specs=hbm,
        scratch_shapes=[pltpu.VMEM((2, ROWS, LANES), f32), dma((2 * NFLD,))],
        name="store",
    )(fields, forcing)
    return out.reshape(1, NFLD, LEV, ROWS * LANES)


def solution(mesh):
    return jax.shard_map(
        functools.partial(per_device, mesh.shape["cells"]),
        mesh=mesh,
        in_specs=(
            P("group", None, None, "cells"),
            P("group", None, "cells"),
            P("group", None, "cells"),
            P("group", None, "cells"),
            P("cells"),
            P("group", None, "cells", None),
            P("group", "cells", None),
            P("group", "cells", None),
        ),
        out_specs=P("group", None, None, "cells"),
        check_vma=False,
    )
```

```python
import functools

import jax
import jax.numpy as jnp
from jax import lax
from jax.experimental import pallas as pl
from jax.experimental.pallas import tpu as pltpu
from jax.sharding import PartitionSpec as P

LANES = 128
LEV = 90
NFLD = 3
ROWS = 32
TOP = 8
RIM = 2
BATCH = 45
SLAB = 12
SLAB_STEP = 10
STRIPS = 3
MESH = pl.DeviceIdType.MESH


def lane_gather(values, index):
    return jnp.take_along_axis(values, index, axis=1, mode="promise_in_bounds")


def window_pair(rows, shift, lane):
    turned = [pltpu.roll(row, lax.rem(LANES - shift, LANES), 1) for row in rows]
    inside = lane < LANES - shift
    return [jnp.where(inside, turned[i], turned[i + 1]) for i in range(2)]


def placed(parts, first_row, shift, lane, row_of):
    turned = [pltpu.roll(part, shift, 1) for part in parts]
    late = lane >= shift
    zero = jnp.zeros_like(turned[0])
    pieces = [
        jnp.where(late, turned[0], zero),
        jnp.where(late, turned[1], turned[0]),
        jnp.where(late, zero, turned[1]),
    ]
    total = jnp.zeros(row_of.shape, jnp.float32)
    for step, piece in enumerate(pieces):
        total = jnp.where(row_of == first_row + step, piece, total)
    return total


def window_kernel(
    n_cells,
    state,
    mixing_hbm,
    weight_hbm,
    place_hbm,
    sea_hbm,
    remap_hbm,
    offsets_hbm,
    live_hbm,
    out,
    flux,
    weight,
    place,
    sea_int,
    remap,
    offsets,
    live,
    first,
    second,
    mixing,
    sea_out,
    sea_in,
    near_air,
    term_out,
    term_in,
    load_sem,
    halo_send,
    halo_recv,
    sea_send,
    sea_recv,
    term_send,
    term_recv,
):
    cell = lax.axis_index("cells")
    group = lax.axis_index("group")
    right = lax.rem(cell + 1, n_cells)
    left = lax.rem(cell + n_cells - 1, n_cells)
    is_ocean = group == STRIPS

    def levels_of(field):
        return pl.ds(field * LEV, LEV)

    def load_of(field):
        return pltpu.make_async_copy(
            state.at[levels_of(field)],
            first.at[levels_of(field), pl.ds(TOP, ROWS), :],
            load_sem.at[field],
        )

    surface = (sea_hbm, sea_int), (place_hbm, place), (weight_hbm, weight), (mixing_hbm, mixing)
    coupling = (remap_hbm, remap), (offsets_hbm, offsets), (live_hbm, live)
    others = [
        pltpu.make_async_copy(source, target, load_sem.at[NFLD + i])
        for i, (source, target) in enumerate(surface + coupling)
    ]
    for field in range(NFLD):
        load_of(field).start()
    for copy in others:
        copy.start()

    barrier = pltpu.get_barrier_semaphore()
    for device in (left, right):
        pl.semaphore_signal(barrier, inc=1, device_id=(group, device), device_id_type=MESH)

    @pl.when(is_ocean)
    def _():
        for strip in range(STRIPS):
            for device in (cell, right):
                pl.semaphore_signal(barrier, inc=1, device_id=(strip, device), device_id_type=MESH)
        pl.semaphore_wait(barrier, 2 + 2 * STRIPS)

    @pl.when(jnp.logical_not(is_ocean))
    def _():
        for device in (cell, left):
            pl.semaphore_signal(barrier, inc=1, device_id=(STRIPS, device), device_id_type=MESH)
        pl.semaphore_wait(barrier, 4)

    def halo(step, field, side):
        levels = levels_of(field)
        if step == 0:
            source, low, high, target = state, 0, ROWS - RIM, first
        else:
            source, low, high, target = second, TOP, TOP + ROWS - RIM, second
        if side == 0:
            begin, land, device = high, TOP - RIM, right
        else:
            begin, land, device = low, TOP + ROWS, left
        return pltpu.make_async_remote_copy(
            src_ref=source.at[levels, pl.ds(begin, RIM), :],
            dst_ref=target.at[levels, pl.ds(land, RIM), :],
            send_sem=halo_send.at[step, side, field],
            recv_sem=halo_recv.at[step, side, field],
            device_id=(group, device),
            device_id_type=MESH,
        )

    for field in range(NFLD):
        for side in range(2):
            halo(0, field, side).start()

    def sea_copy(strip, pair):
        return pltpu.make_async_remote_copy(
            src_ref=sea_out.at[:, pl.ds(strip * SLAB_STEP, SLAB), :],
            dst_ref=sea_in.at[pair, :, pl.ds(0, SLAB), :],
            send_sem=sea_send.at[strip, pair],
            recv_sem=sea_recv.at[pair],
            device_id=(strip, (cell, right)[pair]),
            device_id_type=MESH,
        )

    def term_copy(strip, pair):
        return pltpu.make_async_remote_copy(
            src_ref=term_out.at[pair],
            dst_ref=term_in.at[strip, pair],
            send_sem=term_send.at[pair],
            recv_sem=term_recv.at[strip, pair],
            device_id=(STRIPS, (cell, left)[pair]),
            device_id_type=MESH,
        )

    for field in range(NFLD):
        load_of(field).wait()
    for copy in others:
        copy.wait()
    sea_mask = sea_int[...].astype(jnp.float32)

    @pl.when(is_ocean)
    def _():
        for field in range(2):
            sea_out[field] = first[field * LEV, TOP : TOP + ROWS, :] * sea_mask
        sea_out[2] = sea_mask
        for strip in range(STRIPS):
            for pair in range(2):
                sea_copy(strip, pair).start()

    lane8 = lax.broadcasted_iota(jnp.int32, (8, LANES), 1)
    row8 = lax.broadcasted_iota(jnp.int32, (8, LANES), 0)
    half = lane8 < LANES // 2

    def advance(source, target, target_top, field, chunk):
        rows = slice(chunk * 8, chunk * 8 + 8)
        position = [place[k, rows, :] for k in range(3)]
        index = [p & (LANES - 1) for p in position]
        apart = [(p >> 7) - (row8 + (chunk * 8 + RIM)) for p in position]
        part = [weight[k, rows, :] for k in range(3)]
        centre = part[0] + part[1] + part[2]
        scale = jnp.where(is_ocean, sea_int[rows, :].astype(jnp.float32), 1.0)
        far_at = [apart[2] == g for g in (-2, -1, 1, 2)]
        here = [apart[k] == 0 for k in range(2)]
        base = TOP + chunk * 8
        steps = LEV // BATCH

        def batch(t, carry):
            begin, below = carry
            level = t * BATCH
            at = field * LEV + level
            x = [begin] + [source[at + b, pl.ds(base, 8), :] for b in range(1, BATCH + 1)]
            before = [source[at + b, pl.ds(base - 1, 8), :] for b in range(BATCH)]
            after = [source[at + b, pl.ds(base + 1, 8), :] for b in range(BATCH)]
            mixed = []
            for b in range(BATCH):
                before2 = source[at + b, pl.ds(base - 2, 8), :]
                after2 = source[at + b, pl.ds(base + 2, 8), :]
                value = lane_gather(x[b], index[2])
                for chosen, row in zip(far_at, (before2, before[b], after[b], after2)):
                    value = jnp.where(chosen, lane_gather(row, index[2]), value)
                mixed.append(part[2] * value - centre * x[b])
            edge = [jnp.where(half, after[b], before[b]) for b in range(BATCH)]
            for k in range(2):
                for b in range(BATCH):
                    value = jnp.where(here[k], lane_gather(x[b], index[k]), lane_gather(edge[b], index[k]))
                    mixed[b] = mixed[b] + part[k] * value
            for b in range(BATCH):
                upward = mixing[level + b, rows, :] * (x[b + 1] - x[b])
                if b == BATCH - 1:
                    upward = jnp.where(t == steps - 1, 0.0, upward)
                target[at + b, target_top + chunk * 8 : target_top + chunk * 8 + 8, :] = x[b] + scale * (
                    mixed[b] + (upward - below)
                )
                below = upward
            return x[BATCH], below

        start = source[field * LEV, pl.ds(base, 8), :]
        lax.fori_loop(0, steps, batch, (start, jnp.zeros((8, LANES), jnp.float32)))

    def each_field(body):
        lax.fori_loop(0, NFLD, lambda field, c: (body(field), c)[1], 0)

    def inner_first(field):
        for chunk in (1, 2):
            advance(first, second, TOP, field, chunk)

    each_field(inner_first)

    lane1 = lax.broadcasted_iota(jnp.int32, (1, LANES), 1)
    lane3 = lax.broadcasted_iota(jnp.int32, (3, LANES), 1)
    lane2 = lax.broadcasted_iota(jnp.int32, (2, LANES), 1)
    row_of = lax.broadcasted_iota(jnp.int32, (ROWS, LANES), 0)
    slab_row = lax.broadcasted_iota(jnp.int32, (16, LANES), 0)

    @pl.when(jnp.logical_not(is_ocean))
    def _():
        gap = [jnp.zeros((ROWS, LANES), jnp.float32) for _ in range(2)]
        for field in range(2):
            near_air[field, 0:ROWS, :] = first[field * LEV, TOP : TOP + ROWS, :]
            near_air[field, ROWS:, :] = jnp.zeros((8, LANES), jnp.float32)
        for pair in range(2):
            sea_copy(0, pair).wait_recv()
        for pair in range(2):
            col = offsets[2 * pair]
            row = offsets[2 * pair + 1] - group * (SLAB_STEP * LANES)
            rows_live = live[pair]
            sea = window_pair(
                [sea_in[pair, :, jnp.clip((row >> 7) + i, 0, 15), :] for i in range(3)],
                row & (LANES - 1),
                lane3,
            )
            sea = [jnp.where(lane3 + i * LANES < rows_live, sea[i], 0.0) for i in range(2)]
            moved = jnp.zeros((3, 2 * LANES), jnp.float32)
            for i in range(2):
                moved = moved + jnp.dot(
                    sea[i],
                    remap[pair, i * LANES : (i + 1) * LANES, :],
                    precision=lax.Precision.HIGHEST,
                    preferred_element_type=jnp.float32,
                )
            for field in range(2):
                air = window_pair(
                    [near_air[field, pl.ds(jnp.clip((col >> 7) + i, 0, ROWS), 1), :] for i in range(3)],
                    col & (LANES - 1),
                    lane1,
                )
                parts = [
                    moved[field : field + 1, i * LANES : (i + 1) * LANES]
                    - air[i] * moved[2:3, i * LANES : (i + 1) * LANES]
                    for i in range(2)
                ]
                gap[field] = gap[field] + placed(parts, col >> 7, col & (LANES - 1), lane1, row_of)
        for field in range(2):
            flux[field, 0:ROWS, :] = 0.5 * gap[field]
            flux[field, ROWS:, :] = jnp.zeros((8, LANES), jnp.float32)
        for pair in range(2):
            col = offsets[2 * pair]
            row = offsets[2 * pair + 1] - group * (SLAB_STEP * LANES)
            rows_live = live[pair]
            back = window_pair(
                [flux[:, jnp.clip((col >> 7) + i, 0, ROWS), :] for i in range(3)], col & (LANES - 1), lane2
            )
            parts = []
            for i in range(2):
                block = remap[pair, i * LANES : (i + 1) * LANES, :]
                term = jnp.zeros((2, LANES), jnp.float32)
                for j in range(2):
                    term = term + lax.dot_general(
                        back[j],
                        block[:, j * LANES : (j + 1) * LANES],
                        (((1,), (1,)), ((), ())),
                        precision=lax.Precision.HIGHEST,
                        preferred_element_type=jnp.float32,
                    )
                parts.append(jnp.where(lane2 + i * LANES < rows_live, term, 0.0))
            for field in range(2):
                laid = placed(
                    [part[field : field + 1] for part in parts], row >> 7, row & (LANES - 1), lane1, slab_row
                )
                term_out[pair, field] = laid
        for strip in range(STRIPS):

            @pl.when(group == strip)
            def _():
                for pair in range(2):
                    term_copy(strip, pair).start()

    def outer_first(field):
        for side, chunk in ((0, 0), (1, ROWS // 8 - 1)):
            halo(0, field, side).wait_recv()
            advance(first, second, TOP, field, chunk)
            halo(1, field, 1 - side).start()

    each_field(outer_first)

    def inner_second(field):
        for chunk in (1, 2):
            advance(second, out, 0, field, chunk)

    each_field(inner_second)

    @pl.when(is_ocean)
    def _():
        for field in range(2):
            flux[field] = jnp.zeros((ROWS + 8, LANES), jnp.float32)
        for strip in range(STRIPS):
            for pair in range(2):
                term_copy(strip, pair).wait_recv()
                for field in range(2):
                    at = slice(strip * SLAB_STEP, strip * SLAB_STEP + SLAB)
                    flux[field, at, :] = flux[field, at, :] + term_in[strip, pair, field, 0:SLAB, :]
        for field in range(2):
            flux[field, 0:ROWS, :] = -flux[field, 0:ROWS, :] * sea_mask

    def outer_second(field):
        for side, chunk in ((0, 0), (1, ROWS // 8 - 1)):
            halo(1, field, side).wait_recv()
            advance(second, out, 0, field, chunk)

    each_field(outer_second)

    for step in range(2):
        for field in range(NFLD):
            for side in range(2):
                halo(step, field, side).wait_send()

    @pl.when(is_ocean)
    def _():
        for strip in range(STRIPS):
            for pair in range(2):
                sea_copy(strip, pair).wait_send()

    @pl.when(jnp.logical_not(is_ocean))
    def _():
        for pair in range(2):
            term_copy(0, pair).wait_send()


def store_kernel(fields, forcing, out, top, sem):
    copies = []
    for field in range(NFLD):
        first = field * LEV + (1 if field < 2 else 0)
        rows = pl.ds(first, (field + 1) * LEV - first)
        copies.append(pltpu.make_async_copy(fields.at[rows], out.at[rows], sem.at[field]))
    for copy in copies:
        copy.start()
    for field in range(2):
        top[field] = fields[field * LEV] + forcing[field, 0:ROWS, :]
        copy = pltpu.make_async_copy(top.at[field], out.at[field * LEV], sem.at[NFLD + field])
        copy.start()
        copies.append(copy)
    for copy in copies:
        copy.wait()


def per_device(
    n_cells,
    state,
    vertical_mix,
    neighbour_weight,
    neighbours,
    land_sea,
    remap_weight,
    pair_offsets,
    pair_rows,
):
    hbm = pl.BlockSpec(memory_space=pltpu.HBM)
    vmem = pl.BlockSpec(memory_space=pltpu.VMEM)
    levels = NFLD * LEV
    f32 = jnp.float32
    dma = pltpu.SemaphoreType.DMA
    operands = (
        state.reshape(levels, ROWS, LANES),
        vertical_mix.reshape(LEV, ROWS, LANES),
        neighbour_weight.reshape(3, ROWS, LANES),
        neighbours.reshape(3, ROWS, LANES),
        land_sea.reshape(ROWS, LANES),
        remap_weight[0],
        pair_offsets.reshape(4),
        pair_rows.reshape(2),
    )
    fields, forcing = pl.pallas_call(
        functools.partial(window_kernel, n_cells),
        out_shape=(pltpu.VMEM((levels, ROWS, LANES), f32), pltpu.VMEM((2, ROWS + 8, LANES), f32)),
        in_specs=[hbm] * 8,
        out_specs=(vmem, vmem),
        scratch_shapes=[
            pltpu.VMEM((3, ROWS, LANES), f32),
            pltpu.VMEM((3, ROWS, LANES), jnp.int32),
            pltpu.VMEM((ROWS, LANES), jnp.int32),
            pltpu.VMEM((2, 2 * LANES, 2 * LANES), f32),
            pltpu.SMEM((4,), jnp.int32),
            pltpu.SMEM((2,), jnp.int32),
            pltpu.VMEM((levels + 2, 48, LANES), f32),
            pltpu.VMEM((levels + 2, 48, LANES), f32),
            pltpu.VMEM((LEV, ROWS, LANES), f32),
            pltpu.VMEM((3, ROWS, LANES), f32),
            pltpu.VMEM((2, 3, 16, LANES), f32),
            pltpu.VMEM((2, ROWS + 8, LANES), f32),
            pltpu.VMEM((2, 2, 16, LANES), f32),
            pltpu.VMEM((STRIPS, 2, 2, 16, LANES), f32),
            dma((NFLD + 7,)),
            dma((2, 2, NFLD)),
            dma((2, 2, NFLD)),
            dma((STRIPS, 2)),
            dma((2,)),
            dma((2,)),
            dma((STRIPS, 2)),
        ],
        compiler_params=pltpu.CompilerParams(
            collective_id=0, has_side_effects=True, vmem_limit_bytes=40 * 1024 * 1024
        ),
        name="window",
    )(*(pltpu.with_memory_space_constraint(operand, pltpu.HBM) for operand in operands))
    out = pl.pallas_call(
        store_kernel,
        out_shape=jax.ShapeDtypeStruct((levels, ROWS, LANES), f32),
        in_specs=[vmem, vmem],
        out_specs=hbm,
        scratch_shapes=[pltpu.VMEM((2, ROWS, LANES), f32), dma((2 * NFLD,))],
        compiler_params=pltpu.CompilerParams(vmem_limit_bytes=2 * 1024 * 1024),
        name="store",
    )(fields, forcing)
    return out.reshape(1, NFLD, LEV, ROWS * LANES)


def solution(mesh):
    return jax.shard_map(
        functools.partial(per_device, mesh.shape["cells"]),
        mesh=mesh,
        in_specs=(
            P("group", None, None, "cells"),
            P("group", None, "cells"),
            P("group", None, "cells"),
            P("group", None, "cells"),
            P("cells"),
            P("group", None, "cells", None),
            P("group", "cells", None),
            P("group", "cells", None),
        ),
        out_specs=P("group", None, None, "cells"),
        check_vma=False,
    )
```

```python
import functools

import jax
import jax.numpy as jnp
from jax import lax
from jax.experimental import pallas as pl
from jax.experimental.pallas import tpu as pltpu
from jax.sharding import PartitionSpec as P

LANES = 128
LEV = 90
NFLD = 3
ROWS = 32
TOP = 8
RIM = 2
BATCH = 45
SLAB = 12
SLAB_STEP = 10
STRIPS = 3
MESH = pl.DeviceIdType.MESH


def lane_gather(values, index):
    return jnp.take_along_axis(values, index, axis=1, mode="promise_in_bounds")


def window_pair(rows, shift, lane):
    turned = [pltpu.roll(row, lax.rem(LANES - shift, LANES), 1) for row in rows]
    inside = lane < LANES - shift
    return [jnp.where(inside, turned[i], turned[i + 1]) for i in range(2)]


def placed(parts, first_row, shift, lane, row_of):
    turned = [pltpu.roll(part, shift, 1) for part in parts]
    late = lane >= shift
    zero = jnp.zeros_like(turned[0])
    pieces = [
        jnp.where(late, turned[0], zero),
        jnp.where(late, turned[1], turned[0]),
        jnp.where(late, zero, turned[1]),
    ]
    total = jnp.zeros(row_of.shape, jnp.float32)
    for step, piece in enumerate(pieces):
        total = jnp.where(row_of == first_row + step, piece, total)
    return total


def window_kernel(
    n_cells,
    state,
    mixing_hbm,
    weight_hbm,
    place_hbm,
    sea_hbm,
    remap_hbm,
    offsets_hbm,
    live_hbm,
    out,
    flux,
    weight,
    place,
    sea_int,
    remap,
    offsets,
    live,
    first,
    second,
    rims,
    mixing,
    sea_out,
    sea_in,
    near_air,
    term_out,
    term_in,
    load_sem,
    halo_send,
    halo_recv,
    sea_send,
    sea_recv,
    term_send,
    term_recv,
):
    cell = lax.axis_index("cells")
    group = lax.axis_index("group")
    right = lax.rem(cell + 1, n_cells)
    left = lax.rem(cell + n_cells - 1, n_cells)
    is_ocean = group == STRIPS

    def levels_of(field):
        return pl.ds(field * LEV, LEV)

    def load_of(field):
        return pltpu.make_async_copy(
            state.at[levels_of(field)],
            first.at[levels_of(field), pl.ds(TOP, ROWS), :],
            load_sem.at[field],
        )

    top_rows = [(state.at[field * LEV], near_air.at[field, pl.ds(0, ROWS), :]) for field in range(2)]
    pairs = top_rows + [
        (sea_hbm, sea_int),
        (place_hbm, place),
        (weight_hbm, weight),
        (mixing_hbm, mixing),
        (remap_hbm, remap),
        (offsets_hbm, offsets),
        (live_hbm, live),
    ]
    others = [pltpu.make_async_copy(*pair, load_sem.at[NFLD + i]) for i, pair in enumerate(pairs)]
    for copy in others[:5]:
        copy.start()
    for field in range(NFLD):
        load_of(field).start()
    for copy in others[5:]:
        copy.start()

    barrier = pltpu.get_barrier_semaphore()
    for device in (left, right):
        pl.semaphore_signal(barrier, inc=1, device_id=(group, device), device_id_type=MESH)

    @pl.when(is_ocean)
    def _():
        for strip in range(STRIPS):
            for device in (cell, right):
                pl.semaphore_signal(barrier, inc=1, device_id=(strip, device), device_id_type=MESH)

    @pl.when(jnp.logical_not(is_ocean))
    def _():
        for device in (cell, left):
            pl.semaphore_signal(barrier, inc=1, device_id=(STRIPS, device), device_id_type=MESH)

    def halo(step, field, side):
        levels = levels_of(field)
        source, low = ((state, 0), (second, TOP))[step]
        if side == 0:
            begin, land, device = low + ROWS - RIM, TOP - RIM, right
        else:
            begin, land, device = low, 0, left
        return pltpu.make_async_remote_copy(
            src_ref=source.at[levels, pl.ds(begin, RIM), :],
            dst_ref=rims.at[step, levels, pl.ds(land, RIM), :],
            send_sem=halo_send.at[step, side, field],
            recv_sem=halo_recv.at[step, side, field],
            device_id=(group, device),
            device_id_type=MESH,
        )

    def sea_copy(strip, pair):
        return pltpu.make_async_remote_copy(
            src_ref=sea_out.at[:, pl.ds(strip * SLAB_STEP, SLAB), :],
            dst_ref=sea_in.at[pair, :, pl.ds(0, SLAB), :],
            send_sem=sea_send.at[strip, pair],
            recv_sem=sea_recv.at[pair],
            device_id=(strip, (cell, right)[pair]),
            device_id_type=MESH,
        )

    def term_copy(strip, pair):
        return pltpu.make_async_remote_copy(
            src_ref=term_out.at[pair],
            dst_ref=term_in.at[strip, pair],
            send_sem=term_send.at[pair],
            recv_sem=term_recv.at[strip, pair],
            device_id=(STRIPS, (cell, left)[pair]),
            device_id_type=MESH,
        )

    for copy in others[:3]:
        copy.wait()
    sea_mask = sea_int[...].astype(jnp.float32)

    @pl.when(is_ocean)
    def _():
        for field in range(2):
            sea_out[field] = near_air[field, 0:ROWS, :] * sea_mask
        sea_out[2] = sea_mask
        pl.semaphore_wait(barrier, 2 + 2 * STRIPS)
        for strip in range(STRIPS):
            for pair in range(2):
                sea_copy(strip, pair).start()

    @pl.when(jnp.logical_not(is_ocean))
    def _():
        pl.semaphore_wait(barrier, 4)

    for field in range(NFLD):
        for side in range(2):
            halo(0, field, side).start()
    for copy in others[3:]:
        copy.wait()

    lane8 = lax.broadcasted_iota(jnp.int32, (8, LANES), 1)
    row8 = lax.broadcasted_iota(jnp.int32, (8, LANES), 0)
    half = lane8 < LANES // 2

    upper = row8 < 4

    def advance(source, target, target_top, field, chunks):
        def take(load):
            values = [load(8 * chunk) for chunk in chunks]
            return values[0] if len(values) == 1 else jnp.where(upper, *values)

        own_row = take(lambda row: row8 + (row + RIM))
        position = [take(lambda row: place[k, row : row + 8, :]) for k in range(3)]
        index = [p & (LANES - 1) for p in position]
        apart = [(p >> 7) - own_row for p in position]
        part = [take(lambda row: weight[k, row : row + 8, :]) for k in range(3)]
        centre = part[0] + part[1] + part[2]
        scale = jnp.where(is_ocean, take(lambda row: sea_int[row : row + 8, :]).astype(jnp.float32), 1.0)
        far_at = [apart[2] == g for g in (-2, -1, 1, 2)]
        here = [apart[k] == 0 for k in range(2)]
        steps = LEV // BATCH

        def batch(t, carry):
            begin, below = carry
            level = t * BATCH
            at = field * LEV + level

            def rows_at(b, shift):
                return take(lambda row: source[at + b, pl.ds(TOP + row + shift, 8), :])

            x = [begin] + [rows_at(b, 0) for b in range(1, BATCH)]
            x.append(rows_at(jnp.minimum(BATCH, LEV - 1 - level), 0))
            before = [rows_at(b, -1) for b in range(BATCH)]
            after = [rows_at(b, 1) for b in range(BATCH)]
            mixed = []
            for b in range(BATCH):
                before2 = rows_at(b, -2)
                after2 = rows_at(b, 2)
                value = lane_gather(x[b], index[2])
                for chosen, row in zip(far_at, (before2, before[b], after[b], after2)):
                    value = jnp.where(chosen, lane_gather(row, index[2]), value)
                mixed.append(part[2] * value - centre * x[b])
            edge = [jnp.where(half, after[b], before[b]) for b in range(BATCH)]
            for k in range(2):
                for b in range(BATCH):
                    value = jnp.where(here[k], lane_gather(x[b], index[k]), lane_gather(edge[b], index[k]))
                    mixed[b] = mixed[b] + part[k] * value
            for b in range(BATCH):
                upward = take(lambda row: mixing[level + b, row : row + 8, :]) * (x[b + 1] - x[b])
                if b == BATCH - 1:
                    upward = jnp.where(t == steps - 1, 0.0, upward)
                result = x[b] + scale * (mixed[b] + (upward - below))
                for i, chunk in enumerate(chunks):
                    low, high = (0, 8) if len(chunks) == 1 else (4 * i, 4 * i + 4)
                    row = target_top + 8 * chunk
                    target[at + b, row + low : row + high, :] = result[low:high]
                below = upward
            return x[BATCH], below

        start = take(lambda row: source[field * LEV, pl.ds(TOP + row, 8), :])
        lax.fori_loop(0, steps, batch, (start, jnp.zeros((8, LANES), jnp.float32)))

    last = ROWS // 8 - 1

    def inner(source, target, target_top, field):
        for chunks in ((1,), (2,), (last, 0)):
            advance(source, target, target_top, field, chunks)

    def outer(step, source, target, target_top, field):
        for side in range(2):
            halo(step, field, side).wait_recv()

        def land(i, c):
            for b in range(10):
                at = field * LEV + i * 10 + b
                source[at, TOP - RIM : TOP, :] = rims[step, at, TOP - RIM : TOP, :]
                source[at, TOP + ROWS : TOP + ROWS + RIM, :] = rims[step, at, 0:RIM, :]
            return c

        lax.fori_loop(0, LEV // 10, land, 0)
        advance(source, target, target_top, field, (0, last))

    def first_section(turn, c):
        @pl.when(turn < NFLD)
        def _():
            load_of(turn).wait()
            inner(first, second, TOP, turn)

        @pl.when(turn >= 1)
        def _():
            field = turn - 1
            outer(0, first, second, TOP, field)
            for side in range(2):
                halo(1, field, side).start()

        return c

    lax.fori_loop(0, NFLD + 1, first_section, 0)

    lane1 = lax.broadcasted_iota(jnp.int32, (1, LANES), 1)
    lane3 = lax.broadcasted_iota(jnp.int32, (3, LANES), 1)
    lane2 = lax.broadcasted_iota(jnp.int32, (2, LANES), 1)
    row_of = lax.broadcasted_iota(jnp.int32, (ROWS, LANES), 0)
    slab_row = lax.broadcasted_iota(jnp.int32, (16, LANES), 0)

    @pl.when(jnp.logical_not(is_ocean))
    def _():
        gap = [jnp.zeros((ROWS, LANES), jnp.float32) for _ in range(2)]
        for field in range(2):
            near_air[field, ROWS:, :] = jnp.zeros((8, LANES), jnp.float32)
        for pair in range(2):
            sea_copy(0, pair).wait_recv()
        for pair in range(2):
            col = offsets[2 * pair]
            row = offsets[2 * pair + 1] - group * (SLAB_STEP * LANES)
            rows_live = live[pair]
            sea = window_pair(
                [sea_in[pair, :, jnp.clip((row >> 7) + i, 0, 15), :] for i in range(3)],
                row & (LANES - 1),
                lane3,
            )
            sea = [jnp.where(lane3 + i * LANES < rows_live, sea[i], 0.0) for i in range(2)]
            moved = jnp.zeros((3, 2 * LANES), jnp.float32)
            for i in range(2):
                moved = moved + jnp.dot(
                    sea[i],
                    remap[pair, i * LANES : (i + 1) * LANES, :],
                    precision=lax.Precision.HIGHEST,
                    preferred_element_type=jnp.float32,
                )
            for field in range(2):
                air = window_pair(
                    [near_air[field, pl.ds(jnp.clip((col >> 7) + i, 0, ROWS), 1), :] for i in range(3)],
                    col & (LANES - 1),
                    lane1,
                )
                parts = [
                    moved[field : field + 1, i * LANES : (i + 1) * LANES]
                    - air[i] * moved[2:3, i * LANES : (i + 1) * LANES]
                    for i in range(2)
                ]
                gap[field] = gap[field] + placed(parts, col >> 7, col & (LANES - 1), lane1, row_of)
        for field in range(2):
            flux[field, 0:ROWS, :] = 0.5 * gap[field]
            flux[field, ROWS:, :] = jnp.zeros((8, LANES), jnp.float32)
        for pair in range(2):
            col = offsets[2 * pair]
            row = offsets[2 * pair + 1] - group * (SLAB_STEP * LANES)
            rows_live = live[pair]
            back = window_pair(
                [flux[:, jnp.clip((col >> 7) + i, 0, ROWS), :] for i in range(3)], col & (LANES - 1), lane2
            )
            parts = []
            for i in range(2):
                block = remap[pair, i * LANES : (i + 1) * LANES, :]
                term = jnp.zeros((2, LANES), jnp.float32)
                for j in range(2):
                    term = term + lax.dot_general(
                        back[j],
                        block[:, j * LANES : (j + 1) * LANES],
                        (((1,), (1,)), ((), ())),
                        precision=lax.Precision.HIGHEST,
                        preferred_element_type=jnp.float32,
                    )
                parts.append(jnp.where(lane2 + i * LANES < rows_live, term, 0.0))
            for field in range(2):
                laid = placed(
                    [part[field : field + 1] for part in parts], row >> 7, row & (LANES - 1), lane1, slab_row
                )
                term_out[pair, field] = laid
        for strip in range(STRIPS):

            @pl.when(group == strip)
            def _():
                for pair in range(2):
                    term_copy(strip, pair).start()

    def inner_second(field, c):
        inner(second, out, 0, field)
        return c

    lax.fori_loop(0, NFLD, inner_second, 0)

    @pl.when(is_ocean)
    def _():
        for field in range(2):
            flux[field] = jnp.zeros((ROWS + 8, LANES), jnp.float32)
        for strip in range(STRIPS):
            for pair in range(2):
                term_copy(strip, pair).wait_recv()
                for field in range(2):
                    at = slice(strip * SLAB_STEP, strip * SLAB_STEP + SLAB)
                    flux[field, at, :] = flux[field, at, :] + term_in[strip, pair, field, 0:SLAB, :]
        for field in range(2):
            flux[field, 0:ROWS, :] = -flux[field, 0:ROWS, :] * sea_mask

    def outer_second(field, c):
        outer(1, second, out, 0, field)
        return c

    lax.fori_loop(0, NFLD, outer_second, 0)

    for step in range(2):
        for field in range(NFLD):
            for side in range(2):
                halo(step, field, side).wait_send()

    @pl.when(is_ocean)
    def _():
        for strip in range(STRIPS):
            for pair in range(2):
                sea_copy(strip, pair).wait_send()

    @pl.when(jnp.logical_not(is_ocean))
    def _():
        for pair in range(2):
            term_copy(0, pair).wait_send()


def store_kernel(fields, forcing, out, top, sem):
    copies = []
    for field in range(NFLD):
        first = field * LEV + (1 if field < 2 else 0)
        rows = pl.ds(first, (field + 1) * LEV - first)
        copies.append(pltpu.make_async_copy(fields.at[rows], out.at[rows], sem.at[field]))
    for copy in copies:
        copy.start()
    for field in range(2):
        top[field] = fields[field * LEV] + forcing[field, 0:ROWS, :]
        copy = pltpu.make_async_copy(top.at[field], out.at[field * LEV], sem.at[NFLD + field])
        copy.start()
        copies.append(copy)
    for copy in copies:
        copy.wait()


def per_device(
    n_cells,
    state,
    vertical_mix,
    neighbour_weight,
    neighbours,
    land_sea,
    remap_weight,
    pair_offsets,
    pair_rows,
):
    hbm = pl.BlockSpec(memory_space=pltpu.HBM)
    vmem = pl.BlockSpec(memory_space=pltpu.VMEM)
    levels = NFLD * LEV
    f32 = jnp.float32
    dma = pltpu.SemaphoreType.DMA
    operands = (
        state.reshape(levels, ROWS, LANES),
        vertical_mix.reshape(LEV, ROWS, LANES),
        neighbour_weight.reshape(3, ROWS, LANES),
        neighbours.reshape(3, ROWS, LANES),
        land_sea.reshape(ROWS, LANES),
        remap_weight[0],
        pair_offsets.reshape(4),
        pair_rows.reshape(2),
    )
    fields, forcing = pl.pallas_call(
        functools.partial(window_kernel, n_cells),
        out_shape=(pltpu.VMEM((levels, ROWS, LANES), f32), pltpu.VMEM((2, ROWS + 8, LANES), f32)),
        in_specs=[hbm] * 8,
        out_specs=(vmem, vmem),
        scratch_shapes=[
            pltpu.VMEM((3, ROWS, LANES), f32),
            pltpu.VMEM((3, ROWS, LANES), jnp.int32),
            pltpu.VMEM((ROWS, LANES), jnp.int32),
            pltpu.VMEM((2, 2 * LANES, 2 * LANES), f32),
            pltpu.SMEM((4,), jnp.int32),
            pltpu.SMEM((2,), jnp.int32),
            pltpu.VMEM((levels + 2, 48, LANES), f32),
            pltpu.VMEM((levels + 2, 48, LANES), f32),
            pltpu.VMEM((2, levels, 8, LANES), f32),
            pltpu.VMEM((LEV, ROWS, LANES), f32),
            pltpu.VMEM((3, ROWS, LANES), f32),
            pltpu.VMEM((2, 3, 16, LANES), f32),
            pltpu.VMEM((2, ROWS + 8, LANES), f32),
            pltpu.VMEM((2, 2, 16, LANES), f32),
            pltpu.VMEM((STRIPS, 2, 2, 16, LANES), f32),
            dma((NFLD + 9,)),
            dma((2, 2, NFLD)),
            dma((2, 2, NFLD)),
            dma((STRIPS, 2)),
            dma((2,)),
            dma((2,)),
            dma((STRIPS, 2)),
        ],
        compiler_params=pltpu.CompilerParams(
            collective_id=0, has_side_effects=True, vmem_limit_bytes=40 * 1024 * 1024
        ),
        name="window",
    )(*(pltpu.with_memory_space_constraint(operand, pltpu.HBM) for operand in operands))
    out = pl.pallas_call(
        store_kernel,
        out_shape=jax.ShapeDtypeStruct((levels, ROWS, LANES), f32),
        in_specs=[vmem, vmem],
        out_specs=hbm,
        scratch_shapes=[pltpu.VMEM((2, ROWS, LANES), f32), dma((2 * NFLD,))],
        compiler_params=pltpu.CompilerParams(vmem_limit_bytes=2 * 1024 * 1024),
        name="store",
    )(fields, forcing)
    return out.reshape(1, NFLD, LEV, ROWS * LANES)


def solution(mesh):
    return jax.shard_map(
        functools.partial(per_device, mesh.shape["cells"]),
        mesh=mesh,
        in_specs=(
            P("group", None, None, "cells"),
            P("group", None, "cells"),
            P("group", None, "cells"),
            P("group", None, "cells"),
            P("cells"),
            P("group", None, "cells", None),
            P("group", "cells", None),
            P("group", "cells", None),
        ),
        out_specs=P("group", None, None, "cells"),
        check_vma=False,
    )
```

```python
import functools

import jax
import jax.numpy as jnp
from jax import lax
from jax.experimental import pallas as pl
from jax.experimental.pallas import tpu as pltpu
from jax.sharding import PartitionSpec as P

LANES = 128
LEV = 90
NFLD = 3
ROWS = 32
TOP = 8
RIM = 2
BATCH = 45
SLAB = 12
SLAB_STEP = 10
STRIPS = 3
MESH = pl.DeviceIdType.MESH


def lane_gather(values, index):
    return jnp.take_along_axis(values, index, axis=1, mode="promise_in_bounds")


def window_pair(rows, shift, lane):
    turned = [pltpu.roll(row, lax.rem(LANES - shift, LANES), 1) for row in rows]
    inside = lane < LANES - shift
    return [jnp.where(inside, turned[i], turned[i + 1]) for i in range(2)]


def placed(parts, first_row, shift, lane, row_of):
    turned = [pltpu.roll(part, shift, 1) for part in parts]
    late = lane >= shift
    zero = jnp.zeros_like(turned[0])
    pieces = [
        jnp.where(late, turned[0], zero),
        jnp.where(late, turned[1], turned[0]),
        jnp.where(late, zero, turned[1]),
    ]
    total = jnp.zeros(row_of.shape, jnp.float32)
    for step, piece in enumerate(pieces):
        total = jnp.where(row_of == first_row + step, piece, total)
    return total


def window_kernel(
    n_cells,
    state,
    mixing_hbm,
    weight_hbm,
    place_hbm,
    sea_hbm,
    remap_hbm,
    offsets_hbm,
    live_hbm,
    out,
    flux,
    weight,
    place,
    sea_int,
    remap,
    offsets,
    live,
    first,
    second,
    rims,
    mixing,
    sea_out,
    sea_in,
    near_air,
    term_out,
    term_in,
    load_sem,
    halo_send,
    halo_recv,
    sea_send,
    sea_recv,
    term_send,
    term_recv,
):
    cell = lax.axis_index("cells")
    group = lax.axis_index("group")
    right = lax.rem(cell + 1, n_cells)
    left = lax.rem(cell + n_cells - 1, n_cells)
    is_ocean = group == STRIPS

    def levels_of(field):
        return pl.ds(field * LEV, LEV)

    def load_of(field):
        return pltpu.make_async_copy(
            state.at[levels_of(field)],
            first.at[levels_of(field), pl.ds(TOP, ROWS), :],
            load_sem.at[field],
        )

    top_rows = [(state.at[field * LEV], near_air.at[field, pl.ds(0, ROWS), :]) for field in range(2)]
    pairs = top_rows + [
        (sea_hbm, sea_int),
        (place_hbm, place),
        (weight_hbm, weight),
        (mixing_hbm, mixing),
        (remap_hbm, remap),
        (offsets_hbm, offsets),
        (live_hbm, live),
    ]
    others = [pltpu.make_async_copy(*pair, load_sem.at[NFLD + i]) for i, pair in enumerate(pairs)]
    for copy in others[:5]:
        copy.start()
    for field in range(NFLD):
        load_of(field).start()
    for copy in others[5:]:
        copy.start()

    barrier = pltpu.get_barrier_semaphore()
    for device in (left, right):
        pl.semaphore_signal(barrier, inc=1, device_id=(group, device), device_id_type=MESH)

    @pl.when(is_ocean)
    def _():
        for strip in range(STRIPS):
            for device in (cell, right):
                pl.semaphore_signal(barrier, inc=1, device_id=(strip, device), device_id_type=MESH)

    @pl.when(jnp.logical_not(is_ocean))
    def _():
        for device in (cell, left):
            pl.semaphore_signal(barrier, inc=1, device_id=(STRIPS, device), device_id_type=MESH)

    def halo(step, field, side):
        levels = levels_of(field)
        source, low = ((state, 0), (second, TOP))[step]
        if side == 0:
            begin, land, device = low + ROWS - RIM, TOP - RIM, right
        else:
            begin, land, device = low, 0, left
        return pltpu.make_async_remote_copy(
            src_ref=source.at[levels, pl.ds(begin, RIM), :],
            dst_ref=rims.at[step, levels, pl.ds(land, RIM), :],
            send_sem=halo_send.at[step, side, field],
            recv_sem=halo_recv.at[step, side, field],
            device_id=(group, device),
            device_id_type=MESH,
        )

    def sea_copy(strip, pair):
        return pltpu.make_async_remote_copy(
            src_ref=sea_out.at[:, pl.ds(strip * SLAB_STEP, SLAB), :],
            dst_ref=sea_in.at[pair, :, pl.ds(0, SLAB), :],
            send_sem=sea_send.at[strip, pair],
            recv_sem=sea_recv.at[pair],
            device_id=(strip, (cell, right)[pair]),
            device_id_type=MESH,
        )

    def term_copy(strip, pair):
        return pltpu.make_async_remote_copy(
            src_ref=term_out.at[pair],
            dst_ref=term_in.at[strip, pair],
            send_sem=term_send.at[pair],
            recv_sem=term_recv.at[strip, pair],
            device_id=(STRIPS, (cell, left)[pair]),
            device_id_type=MESH,
        )

    for copy in others[:3]:
        copy.wait()
    sea_mask = sea_int[...].astype(jnp.float32)

    @pl.when(is_ocean)
    def _():
        for field in range(2):
            sea_out[field] = near_air[field, 0:ROWS, :] * sea_mask
        sea_out[2] = sea_mask
        pl.semaphore_wait(barrier, 2 + 2 * STRIPS)
        for strip in range(STRIPS):
            for pair in range(1):
                sea_copy(strip, pair).start()

    @pl.when(jnp.logical_not(is_ocean))
    def _():
        pl.semaphore_wait(barrier, 4)

    for field in range(NFLD):
        for side in range(2):
            halo(0, field, side).start()
    @pl.when(is_ocean)
    def _():
        for strip in range(STRIPS):
            for pair in range(1, 2):
                sea_copy(strip, pair).start()
    for copy in others[3:]:
        copy.wait()

    lane8 = lax.broadcasted_iota(jnp.int32, (8, LANES), 1)
    row8 = lax.broadcasted_iota(jnp.int32, (8, LANES), 0)
    half = lane8 < LANES // 2

    upper = row8 < 4

    def advance(source, target, target_top, field, chunks):
        def take(load):
            values = [load(8 * chunk) for chunk in chunks]
            return values[0] if len(values) == 1 else jnp.where(upper, *values)

        own_row = take(lambda row: row8 + (row + RIM))
        position = [take(lambda row: place[k, row : row + 8, :]) for k in range(3)]
        index = [p & (LANES - 1) for p in position]
        apart = [(p >> 7) - own_row for p in position]
        part = [take(lambda row: weight[k, row : row + 8, :]) for k in range(3)]
        centre = part[0] + part[1] + part[2]
        scale = jnp.where(is_ocean, take(lambda row: sea_int[row : row + 8, :]).astype(jnp.float32), 1.0)
        far_at = [apart[2] == g for g in (-2, -1, 1, 2)]
        here = [apart[k] == 0 for k in range(2)]
        steps = LEV // BATCH

        def batch(t, carry):
            begin, below = carry
            level = t * BATCH
            at = field * LEV + level

            def rows_at(b, shift):
                return take(lambda row: source[at + b, pl.ds(TOP + row + shift, 8), :])

            x = [begin] + [rows_at(b, 0) for b in range(1, BATCH)]
            x.append(rows_at(jnp.minimum(BATCH, LEV - 1 - level), 0))
            before = [rows_at(b, -1) for b in range(BATCH)]
            after = [rows_at(b, 1) for b in range(BATCH)]
            mixed = []
            for b in range(BATCH):
                before2 = rows_at(b, -2)
                after2 = rows_at(b, 2)
                value = lane_gather(x[b], index[2])
                for chosen, row in zip(far_at, (before2, before[b], after[b], after2)):
                    value = jnp.where(chosen, lane_gather(row, index[2]), value)
                mixed.append(part[2] * value - centre * x[b])
            edge = [jnp.where(half, after[b], before[b]) for b in range(BATCH)]
            for k in range(2):
                for b in range(BATCH):
                    value = jnp.where(here[k], lane_gather(x[b], index[k]), lane_gather(edge[b], index[k]))
                    mixed[b] = mixed[b] + part[k] * value
            for b in range(BATCH):
                upward = take(lambda row: mixing[level + b, row : row + 8, :]) * (x[b + 1] - x[b])
                if b == BATCH - 1:
                    upward = jnp.where(t == steps - 1, 0.0, upward)
                result = x[b] + scale * (mixed[b] + (upward - below))
                for i, chunk in enumerate(chunks):
                    low, high = (0, 8) if len(chunks) == 1 else (4 * i, 4 * i + 4)
                    row = target_top + 8 * chunk
                    target[at + b, row + low : row + high, :] = result[low:high]
                below = upward
            return x[BATCH], below

        start = take(lambda row: source[field * LEV, pl.ds(TOP + row, 8), :])
        lax.fori_loop(0, steps, batch, (start, jnp.zeros((8, LANES), jnp.float32)))

    last = ROWS // 8 - 1

    def inner(source, target, target_top, field):
        for chunks in ((1,), (2,), (last, 0)):
            advance(source, target, target_top, field, chunks)

    def outer(step, source, target, target_top, field):
        for side in range(2):
            halo(step, field, side).wait_recv()

        def land(i, c):
            for b in range(10):
                at = field * LEV + i * 10 + b
                source[at, TOP - RIM : TOP, :] = rims[step, at, TOP - RIM : TOP, :]
                source[at, TOP + ROWS : TOP + ROWS + RIM, :] = rims[step, at, 0:RIM, :]
            return c

        lax.fori_loop(0, LEV // 10, land, 0)
        advance(source, target, target_top, field, (0, last))

    lane1 = lax.broadcasted_iota(jnp.int32, (1, LANES), 1)
    lane3 = lax.broadcasted_iota(jnp.int32, (3, LANES), 1)
    lane2 = lax.broadcasted_iota(jnp.int32, (2, LANES), 1)
    row_of = lax.broadcasted_iota(jnp.int32, (ROWS, LANES), 0)
    slab_row = lax.broadcasted_iota(jnp.int32, (16, LANES), 0)

    def couple():
        gap = [jnp.zeros((ROWS, LANES), jnp.float32) for _ in range(2)]
        for field in range(2):
            near_air[field, ROWS:, :] = jnp.zeros((8, LANES), jnp.float32)
        for pair in range(2):
            sea_copy(0, pair).wait_recv()
        for pair in range(2):
            col = offsets[2 * pair]
            row = offsets[2 * pair + 1] - group * (SLAB_STEP * LANES)
            rows_live = live[pair]
            sea = window_pair(
                [sea_in[pair, :, jnp.clip((row >> 7) + i, 0, 15), :] for i in range(3)],
                row & (LANES - 1),
                lane3,
            )
            sea = [jnp.where(lane3 + i * LANES < rows_live, sea[i], 0.0) for i in range(2)]
            moved = jnp.zeros((3, 2 * LANES), jnp.float32)
            for i in range(2):
                moved = moved + jnp.dot(
                    sea[i],
                    remap[pair, i * LANES : (i + 1) * LANES, :],
                    precision=lax.Precision.HIGHEST,
                    preferred_element_type=jnp.float32,
                )
            for field in range(2):
                air = window_pair(
                    [near_air[field, pl.ds(jnp.clip((col >> 7) + i, 0, ROWS), 1), :] for i in range(3)],
                    col & (LANES - 1),
                    lane1,
                )
                parts = [
                    moved[field : field + 1, i * LANES : (i + 1) * LANES]
                    - air[i] * moved[2:3, i * LANES : (i + 1) * LANES]
                    for i in range(2)
                ]
                gap[field] = gap[field] + placed(parts, col >> 7, col & (LANES - 1), lane1, row_of)
        for field in range(2):
            flux[field, 0:ROWS, :] = 0.5 * gap[field]
            flux[field, ROWS:, :] = jnp.zeros((8, LANES), jnp.float32)
        for pair in range(2):
            col = offsets[2 * pair]
            row = offsets[2 * pair + 1] - group * (SLAB_STEP * LANES)
            rows_live = live[pair]
            back = window_pair(
                [flux[:, jnp.clip((col >> 7) + i, 0, ROWS), :] for i in range(3)], col & (LANES - 1), lane2
            )
            parts = []
            for i in range(2):
                block = remap[pair, i * LANES : (i + 1) * LANES, :]
                term = jnp.zeros((2, LANES), jnp.float32)
                for j in range(2):
                    term = term + lax.dot_general(
                        back[j],
                        block[:, j * LANES : (j + 1) * LANES],
                        (((1,), (1,)), ((), ())),
                        precision=lax.Precision.HIGHEST,
                        preferred_element_type=jnp.float32,
                    )
                parts.append(jnp.where(lane2 + i * LANES < rows_live, term, 0.0))
            for field in range(2):
                laid = placed(
                    [part[field : field + 1] for part in parts], row >> 7, row & (LANES - 1), lane1, slab_row
                )
                term_out[pair, field] = laid
        for strip in range(STRIPS):

            @pl.when(group == strip)
            def _():
                for pair in range(2):
                    term_copy(strip, pair).start()

    def first_section(turn, c):
        @pl.when(turn < NFLD)
        def _():
            load_of(turn).wait()
            inner(first, second, TOP, turn)

        @pl.when(turn >= 1)
        def _():
            field = turn - 1
            outer(0, first, second, TOP, field)
            for side in range(2):
                halo(1, field, side).start()

        return c

    lax.fori_loop(0, NFLD + 1, first_section, 0)

    def inner_second(field, c):
        inner(second, out, 0, field)

        @pl.when(jnp.logical_not(is_ocean) & (field == 1))
        def _():
            couple()

        return c

    lax.fori_loop(0, NFLD, inner_second, 0)

    def outer_second(field, c):
        outer(1, second, out, 0, field)
        return c

    lax.fori_loop(0, NFLD, outer_second, 0)

    @pl.when(is_ocean)
    def _():
        for field in range(2):
            flux[field] = jnp.zeros((ROWS + 8, LANES), jnp.float32)
        for strip in range(STRIPS):
            for pair in range(2):
                term_copy(strip, pair).wait_recv()
                for field in range(2):
                    at = slice(strip * SLAB_STEP, strip * SLAB_STEP + SLAB)
                    flux[field, at, :] = flux[field, at, :] + term_in[strip, pair, field, 0:SLAB, :]
        for field in range(2):
            flux[field, 0:ROWS, :] = -flux[field, 0:ROWS, :] * sea_mask

    for step in range(2):
        for field in range(NFLD):
            for side in range(2):
                halo(step, field, side).wait_send()

    @pl.when(is_ocean)
    def _():
        for strip in range(STRIPS):
            for pair in range(2):
                sea_copy(strip, pair).wait_send()

    @pl.when(jnp.logical_not(is_ocean))
    def _():
        for pair in range(2):
            term_copy(0, pair).wait_send()


def store_kernel(fields, forcing, out, top, sem):
    copies = []
    for field in range(NFLD):
        first = field * LEV + (1 if field < 2 else 0)
        rows = pl.ds(first, (field + 1) * LEV - first)
        copies.append(pltpu.make_async_copy(fields.at[rows], out.at[rows], sem.at[field]))
    for copy in copies:
        copy.start()
    for field in range(2):
        top[field] = fields[field * LEV] + forcing[field, 0:ROWS, :]
        copy = pltpu.make_async_copy(top.at[field], out.at[field * LEV], sem.at[NFLD + field])
        copy.start()
        copies.append(copy)
    for copy in copies:
        copy.wait()


def per_device(
    n_cells,
    state,
    vertical_mix,
    neighbour_weight,
    neighbours,
    land_sea,
    remap_weight,
    pair_offsets,
    pair_rows,
):
    hbm = pl.BlockSpec(memory_space=pltpu.HBM)
    vmem = pl.BlockSpec(memory_space=pltpu.VMEM)
    levels = NFLD * LEV
    f32 = jnp.float32
    dma = pltpu.SemaphoreType.DMA
    operands = (
        state.reshape(levels, ROWS, LANES),
        vertical_mix.reshape(LEV, ROWS, LANES),
        neighbour_weight.reshape(3, ROWS, LANES),
        neighbours.reshape(3, ROWS, LANES),
        land_sea.reshape(ROWS, LANES),
        remap_weight[0],
        pair_offsets.reshape(4),
        pair_rows.reshape(2),
    )
    fields, forcing = pl.pallas_call(
        functools.partial(window_kernel, n_cells),
        out_shape=(pltpu.VMEM((levels, ROWS, LANES), f32), pltpu.VMEM((2, ROWS + 8, LANES), f32)),
        in_specs=[hbm] * 8,
        out_specs=(vmem, vmem),
        scratch_shapes=[
            pltpu.VMEM((3, ROWS, LANES), f32),
            pltpu.VMEM((3, ROWS, LANES), jnp.int32),
            pltpu.VMEM((ROWS, LANES), jnp.int32),
            pltpu.VMEM((2, 2 * LANES, 2 * LANES), f32),
            pltpu.SMEM((4,), jnp.int32),
            pltpu.SMEM((2,), jnp.int32),
            pltpu.VMEM((levels + 2, 48, LANES), f32),
            pltpu.VMEM((levels + 2, 48, LANES), f32),
            pltpu.VMEM((2, levels, 8, LANES), f32),
            pltpu.VMEM((LEV, ROWS, LANES), f32),
            pltpu.VMEM((3, ROWS, LANES), f32),
            pltpu.VMEM((2, 3, 16, LANES), f32),
            pltpu.VMEM((2, ROWS + 8, LANES), f32),
            pltpu.VMEM((2, 2, 16, LANES), f32),
            pltpu.VMEM((STRIPS, 2, 2, 16, LANES), f32),
            dma((NFLD + 9,)),
            dma((2, 2, NFLD)),
            dma((2, 2, NFLD)),
            dma((STRIPS, 2)),
            dma((2,)),
            dma((2,)),
            dma((STRIPS, 2)),
        ],
        compiler_params=pltpu.CompilerParams(
            collective_id=0, has_side_effects=True, vmem_limit_bytes=40 * 1024 * 1024
        ),
        name="window",
    )(*(pltpu.with_memory_space_constraint(operand, pltpu.HBM) for operand in operands))
    out = pl.pallas_call(
        store_kernel,
        out_shape=jax.ShapeDtypeStruct((levels, ROWS, LANES), f32),
        in_specs=[vmem, vmem],
        out_specs=hbm,
        scratch_shapes=[pltpu.VMEM((2, ROWS, LANES), f32), dma((2 * NFLD,))],
        compiler_params=pltpu.CompilerParams(vmem_limit_bytes=2 * 1024 * 1024),
        name="store",
    )(fields, forcing)
    return out.reshape(1, NFLD, LEV, ROWS * LANES)


def solution(mesh):
    return jax.shard_map(
        functools.partial(per_device, mesh.shape["cells"]),
        mesh=mesh,
        in_specs=(
            P("group", None, None, "cells"),
            P("group", None, "cells"),
            P("group", None, "cells"),
            P("group", None, "cells"),
            P("cells"),
            P("group", None, "cells", None),
            P("group", "cells", None),
            P("group", "cells", None),
        ),
        out_specs=P("group", None, None, "cells"),
        check_vma=False,
    )
```

```python
import functools

import jax
import jax.numpy as jnp
from jax import lax
from jax.experimental import pallas as pl
from jax.experimental.pallas import tpu as pltpu
from jax.sharding import PartitionSpec as P

LANES = 128
LEV = 90
NFLD = 3
ROWS = 32
TOP = 8
RIM = 2
BATCH = 90
SLAB = 12
SLAB_STEP = 10
STRIPS = 3
MESH = pl.DeviceIdType.MESH


def lane_gather(values, index):
    return jnp.take_along_axis(values, index, axis=1, mode="promise_in_bounds")


def window_pair(rows, shift, lane):
    turned = [pltpu.roll(row, lax.rem(LANES - shift, LANES), 1) for row in rows]
    inside = lane < LANES - shift
    return [jnp.where(inside, turned[i], turned[i + 1]) for i in range(2)]


def placed(parts, first_row, shift, lane, row_of):
    turned = [pltpu.roll(part, shift, 1) for part in parts]
    late = lane >= shift
    zero = jnp.zeros_like(turned[0])
    pieces = [
        jnp.where(late, turned[0], zero),
        jnp.where(late, turned[1], turned[0]),
        jnp.where(late, zero, turned[1]),
    ]
    total = jnp.zeros(row_of.shape, jnp.float32)
    for step, piece in enumerate(pieces):
        total = jnp.where(row_of == first_row + step, piece, total)
    return total


def window_kernel(
    n_cells,
    state,
    mixing_hbm,
    weight_hbm,
    place_hbm,
    sea_hbm,
    remap_hbm,
    offsets_hbm,
    live_hbm,
    out,
    flux,
    weight,
    place,
    sea_int,
    remap,
    offsets,
    live,
    first,
    second,
    rims,
    mixing,
    sea_out,
    sea_in,
    near_air,
    term_out,
    term_in,
    load_sem,
    halo_send,
    halo_recv,
    sea_send,
    sea_recv,
    term_send,
    term_recv,
):
    cell = lax.axis_index("cells")
    group = lax.axis_index("group")
    right = lax.rem(cell + 1, n_cells)
    left = lax.rem(cell + n_cells - 1, n_cells)
    is_ocean = group == STRIPS

    def levels_of(field):
        return pl.ds(field * LEV, LEV)

    def load_of(field):
        return pltpu.make_async_copy(
            state.at[levels_of(field)],
            first.at[levels_of(field), pl.ds(TOP, ROWS), :],
            load_sem.at[field],
        )

    top_rows = [(state.at[field * LEV], near_air.at[field, pl.ds(0, ROWS), :]) for field in range(2)]
    pairs = top_rows + [
        (sea_hbm, sea_int),
        (place_hbm, place),
        (weight_hbm, weight),
        (mixing_hbm, mixing),
        (remap_hbm, remap),
        (offsets_hbm, offsets),
        (live_hbm, live),
    ]
    others = [pltpu.make_async_copy(*pair, load_sem.at[NFLD + i]) for i, pair in enumerate(pairs)]
    for copy in others[:5]:
        copy.start()
    for field in range(NFLD):
        load_of(field).start()
    for copy in others[5:]:
        copy.start()

    barrier = pltpu.get_barrier_semaphore()
    for device in (left, right):
        pl.semaphore_signal(barrier, inc=1, device_id=(group, device), device_id_type=MESH)

    @pl.when(is_ocean)
    def _():
        for strip in range(STRIPS):
            for device in (cell, right):
                pl.semaphore_signal(barrier, inc=1, device_id=(strip, device), device_id_type=MESH)

    @pl.when(jnp.logical_not(is_ocean))
    def _():
        for device in (cell, left):
            pl.semaphore_signal(barrier, inc=1, device_id=(STRIPS, device), device_id_type=MESH)

    def halo(step, field, side):
        levels = levels_of(field)
        source, low = ((state, 0), (second, TOP))[step]
        if side == 0:
            begin, land, device = low + ROWS - RIM, TOP - RIM, right
        else:
            begin, land, device = low, 0, left
        return pltpu.make_async_remote_copy(
            src_ref=source.at[levels, pl.ds(begin, RIM), :],
            dst_ref=rims.at[step, levels, pl.ds(land, RIM), :],
            send_sem=halo_send.at[step, side, field],
            recv_sem=halo_recv.at[step, side, field],
            device_id=(group, device),
            device_id_type=MESH,
        )

    def sea_copy(strip, pair):
        return pltpu.make_async_remote_copy(
            src_ref=sea_out.at[:, pl.ds(strip * SLAB_STEP, SLAB), :],
            dst_ref=sea_in.at[pair, :, pl.ds(0, SLAB), :],
            send_sem=sea_send.at[strip, pair],
            recv_sem=sea_recv.at[pair],
            device_id=(strip, (cell, right)[pair]),
            device_id_type=MESH,
        )

    def term_copy(strip, pair):
        return pltpu.make_async_remote_copy(
            src_ref=term_out.at[pair, :, pl.ds(0, SLAB), :],
            dst_ref=term_in.at[strip, pair, :, pl.ds(0, SLAB), :],
            send_sem=term_send.at[pair],
            recv_sem=term_recv.at[strip, pair],
            device_id=(STRIPS, (cell, left)[pair]),
            device_id_type=MESH,
        )

    for copy in others[:3]:
        copy.wait()
    sea_mask = sea_int[...].astype(jnp.float32)

    @pl.when(is_ocean)
    def _():
        for field in range(2):
            sea_out[field] = near_air[field, 0:ROWS, :] * sea_mask
        sea_out[2] = sea_mask
        pl.semaphore_wait(barrier, 2 + 2 * STRIPS)
        for strip in range(STRIPS):
            for pair in range(1):
                sea_copy(strip, pair).start()

    @pl.when(jnp.logical_not(is_ocean))
    def _():
        pl.semaphore_wait(barrier, 4)

    for field in range(NFLD):
        for side in range(2):
            halo(0, field, side).start()
    @pl.when(is_ocean)
    def _():
        for strip in range(STRIPS):
            for pair in range(1, 2):
                sea_copy(strip, pair).start()
    for copy in others[3:]:
        copy.wait()

    lane8 = lax.broadcasted_iota(jnp.int32, (8, LANES), 1)
    row8 = lax.broadcasted_iota(jnp.int32, (8, LANES), 0)
    half = lane8 < LANES // 2

    upper = row8 < 4

    def advance(source, target, target_top, field, chunks):
        def take(load):
            values = [load(8 * chunk) for chunk in chunks]
            return values[0] if len(values) == 1 else jnp.where(upper, *values)

        own_row = take(lambda row: row8 + (row + RIM))
        position = [take(lambda row: place[k, row : row + 8, :]) for k in range(3)]
        index = [p & (LANES - 1) for p in position]
        apart = [(p >> 7) - own_row for p in position]
        part = [take(lambda row: weight[k, row : row + 8, :]) for k in range(3)]
        centre = part[0] + part[1] + part[2]
        scale = jnp.where(is_ocean, take(lambda row: sea_int[row : row + 8, :]).astype(jnp.float32), 1.0)
        far_at = [apart[2] == g for g in (-2, -1, 1, 2)]
        here = [apart[k] == 0 for k in range(2)]
        steps = LEV // BATCH

        def batch(t, carry):
            begin, below = carry
            level = t * BATCH
            at = field * LEV + level

            def rows_at(b, shift):
                return take(lambda row: source[at + b, pl.ds(TOP + row + shift, 8), :])

            x = [begin] + [rows_at(b, 0) for b in range(1, BATCH)]
            x.append(rows_at(jnp.minimum(BATCH, LEV - 1 - level), 0))
            before = [rows_at(b, -1) for b in range(BATCH)]
            after = [rows_at(b, 1) for b in range(BATCH)]
            mixed = []
            for b in range(BATCH):
                before2 = rows_at(b, -2)
                after2 = rows_at(b, 2)
                value = lane_gather(x[b], index[2])
                for chosen, row in zip(far_at, (before2, before[b], after[b], after2)):
                    value = jnp.where(chosen, lane_gather(row, index[2]), value)
                mixed.append(part[2] * value - centre * x[b])
            edge = [jnp.where(half, after[b], before[b]) for b in range(BATCH)]
            for k in range(2):
                for b in range(BATCH):
                    value = jnp.where(here[k], lane_gather(x[b], index[k]), lane_gather(edge[b], index[k]))
                    mixed[b] = mixed[b] + part[k] * value
            for b in range(BATCH):
                upward = take(lambda row: mixing[level + b, row : row + 8, :]) * (x[b + 1] - x[b])
                if b == BATCH - 1:
                    upward = jnp.where(t == steps - 1, 0.0, upward)
                result = x[b] + scale * (mixed[b] + (upward - below))
                for i, chunk in enumerate(chunks):
                    low, high = (0, 8) if len(chunks) == 1 else (4 * i, 4 * i + 4)
                    row = target_top + 8 * chunk
                    target[at + b, row + low : row + high, :] = result[low:high]
                below = upward
            return x[BATCH], below

        start = take(lambda row: source[field * LEV, pl.ds(TOP + row, 8), :])
        lax.fori_loop(0, steps, batch, (start, jnp.zeros((8, LANES), jnp.float32)))

    last = ROWS // 8 - 1

    def inner(source, target, target_top, field):
        for chunks in ((1,), (2,), (last, 0)):
            advance(source, target, target_top, field, chunks)

    def outer(step, source, target, target_top, field):
        for side in range(2):
            halo(step, field, side).wait_recv()

        def land(i, c):
            for b in range(10):
                at = field * LEV + i * 10 + b
                source[at, TOP - RIM : TOP, :] = rims[step, at, TOP - RIM : TOP, :]
                source[at, TOP + ROWS : TOP + ROWS + RIM, :] = rims[step, at, 0:RIM, :]
            return c

        lax.fori_loop(0, LEV // 10, land, 0)
        advance(source, target, target_top, field, (0, last))

    lane1 = lax.broadcasted_iota(jnp.int32, (1, LANES), 1)
    lane3 = lax.broadcasted_iota(jnp.int32, (3, LANES), 1)
    lane2 = lax.broadcasted_iota(jnp.int32, (2, LANES), 1)
    row_of = lax.broadcasted_iota(jnp.int32, (ROWS, LANES), 0)
    slab_row = lax.broadcasted_iota(jnp.int32, (16, LANES), 0)

    def couple():
        gap = [jnp.zeros((ROWS, LANES), jnp.float32) for _ in range(2)]
        for field in range(2):
            near_air[field, ROWS:, :] = jnp.zeros((8, LANES), jnp.float32)
        for pair in range(2):
            sea_copy(0, pair).wait_recv()
        for pair in range(2):
            col = offsets[2 * pair]
            row = offsets[2 * pair + 1] - group * (SLAB_STEP * LANES)
            rows_live = live[pair]
            sea = window_pair(
                [sea_in[pair, :, jnp.clip((row >> 7) + i, 0, 15), :] for i in range(3)],
                row & (LANES - 1),
                lane3,
            )
            sea = [jnp.where(lane3 + i * LANES < rows_live, sea[i], 0.0) for i in range(2)]
            moved = jnp.dot(
                jnp.concatenate(sea, axis=1),
                remap[pair],
                precision=lax.Precision.HIGHEST,
                preferred_element_type=jnp.float32,
            )
            for field in range(2):
                air = window_pair(
                    [near_air[field, pl.ds(jnp.clip((col >> 7) + i, 0, ROWS), 1), :] for i in range(3)],
                    col & (LANES - 1),
                    lane1,
                )
                parts = [
                    moved[field : field + 1, i * LANES : (i + 1) * LANES]
                    - air[i] * moved[2:3, i * LANES : (i + 1) * LANES]
                    for i in range(2)
                ]
                gap[field] = gap[field] + placed(parts, col >> 7, col & (LANES - 1), lane1, row_of)
        for field in range(2):
            flux[field, 0:ROWS, :] = 0.5 * gap[field]
            flux[field, ROWS:, :] = jnp.zeros((8, LANES), jnp.float32)
        for pair in range(2):
            col = offsets[2 * pair]
            row = offsets[2 * pair + 1] - group * (SLAB_STEP * LANES)
            rows_live = live[pair]
            back = window_pair(
                [flux[:, jnp.clip((col >> 7) + i, 0, ROWS), :] for i in range(3)], col & (LANES - 1), lane2
            )
            term = lax.dot_general(
                jnp.concatenate(back, axis=1),
                remap[pair],
                (((1,), (1,)), ((), ())),
                precision=lax.Precision.HIGHEST,
                preferred_element_type=jnp.float32,
            )
            parts = [
                jnp.where(lane2 + i * LANES < rows_live, term[:, i * LANES : (i + 1) * LANES], 0.0)
                for i in range(2)
            ]
            for field in range(2):
                laid = placed(
                    [part[field : field + 1] for part in parts], row >> 7, row & (LANES - 1), lane1, slab_row
                )
                term_out[pair, field] = laid
        for strip in range(STRIPS):

            @pl.when(group == strip)
            def _():
                for pair in range(2):
                    term_copy(strip, pair).start()

    def first_section(turn, c):
        @pl.when(turn < NFLD)
        def _():
            load_of(turn).wait()
            inner(first, second, TOP, turn)

        @pl.when(turn >= 1)
        def _():
            field = turn - 1
            outer(0, first, second, TOP, field)
            for side in range(2):
                halo(1, field, side).start()

        return c

    lax.fori_loop(0, NFLD + 1, first_section, 0)

    def inner_second(field, c):
        for order, chunks in enumerate(((1,), (2,), (last, 0))):
            advance(second, out, 0, field, chunks)
            if order == 0:

                @pl.when(jnp.logical_not(is_ocean) & (field == 2))
                def _():
                    couple()

        return c

    lax.fori_loop(0, NFLD, inner_second, 0)

    def outer_second(field, c):
        outer(1, second, out, 0, field)
        return c

    lax.fori_loop(0, NFLD, outer_second, 0)

    @pl.when(is_ocean)
    def _():
        for field in range(2):
            flux[field] = jnp.zeros((ROWS + 8, LANES), jnp.float32)
        for strip in range(STRIPS):
            for pair in range(2):
                term_copy(strip, pair).wait_recv()
                for field in range(2):
                    at = slice(strip * SLAB_STEP, strip * SLAB_STEP + SLAB)
                    flux[field, at, :] = flux[field, at, :] + term_in[strip, pair, field, 0:SLAB, :]
        for field in range(2):
            flux[field, 0:ROWS, :] = -flux[field, 0:ROWS, :] * sea_mask

    for step in range(2):
        for field in range(NFLD):
            for side in range(2):
                halo(step, field, side).wait_send()

    @pl.when(is_ocean)
    def _():
        for strip in range(STRIPS):
            for pair in range(2):
                sea_copy(strip, pair).wait_send()

    @pl.when(jnp.logical_not(is_ocean))
    def _():
        for pair in range(2):
            term_copy(0, pair).wait_send()


def store_kernel(fields, forcing, out, top, sem):
    copies = []
    for field in range(NFLD):
        first = field * LEV + (1 if field < 2 else 0)
        rows = pl.ds(first, (field + 1) * LEV - first)
        copies.append(pltpu.make_async_copy(fields.at[rows], out.at[rows], sem.at[field]))
    for copy in copies:
        copy.start()
    for field in range(2):
        top[field] = fields[field * LEV] + forcing[field, 0:ROWS, :]
        copy = pltpu.make_async_copy(top.at[field], out.at[field * LEV], sem.at[NFLD + field])
        copy.start()
        copies.append(copy)
    for copy in copies:
        copy.wait()


def per_device(
    n_cells,
    state,
    vertical_mix,
    neighbour_weight,
    neighbours,
    land_sea,
    remap_weight,
    pair_offsets,
    pair_rows,
):
    hbm = pl.BlockSpec(memory_space=pltpu.HBM)
    vmem = pl.BlockSpec(memory_space=pltpu.VMEM)
    levels = NFLD * LEV
    f32 = jnp.float32
    dma = pltpu.SemaphoreType.DMA
    operands = (
        state.reshape(levels, ROWS, LANES),
        vertical_mix.reshape(LEV, ROWS, LANES),
        neighbour_weight.reshape(3, ROWS, LANES),
        neighbours.reshape(3, ROWS, LANES),
        land_sea.reshape(ROWS, LANES),
        remap_weight[0],
        pair_offsets.reshape(4),
        pair_rows.reshape(2),
    )
    fields, forcing = pl.pallas_call(
        functools.partial(window_kernel, n_cells),
        out_shape=(pltpu.VMEM((levels, ROWS, LANES), f32), pltpu.VMEM((2, ROWS + 8, LANES), f32)),
        in_specs=[hbm] * 8,
        out_specs=(vmem, vmem),
        scratch_shapes=[
            pltpu.VMEM((3, ROWS, LANES), f32),
            pltpu.VMEM((3, ROWS, LANES), jnp.int32),
            pltpu.VMEM((ROWS, LANES), jnp.int32),
            pltpu.VMEM((2, 2 * LANES, 2 * LANES), f32),
            pltpu.SMEM((4,), jnp.int32),
            pltpu.SMEM((2,), jnp.int32),
            pltpu.VMEM((levels + 2, 48, LANES), f32),
            pltpu.VMEM((levels + 2, 48, LANES), f32),
            pltpu.VMEM((2, levels, 8, LANES), f32),
            pltpu.VMEM((LEV, ROWS, LANES), f32),
            pltpu.VMEM((3, ROWS, LANES), f32),
            pltpu.VMEM((2, 3, 16, LANES), f32),
            pltpu.VMEM((2, ROWS + 8, LANES), f32),
            pltpu.VMEM((2, 2, 16, LANES), f32),
            pltpu.VMEM((STRIPS, 2, 2, 16, LANES), f32),
            dma((NFLD + 9,)),
            dma((2, 2, NFLD)),
            dma((2, 2, NFLD)),
            dma((STRIPS, 2)),
            dma((2,)),
            dma((2,)),
            dma((STRIPS, 2)),
        ],
        compiler_params=pltpu.CompilerParams(
            collective_id=0, has_side_effects=True, vmem_limit_bytes=40 * 1024 * 1024
        ),
        name="window",
    )(*(pltpu.with_memory_space_constraint(operand, pltpu.HBM) for operand in operands))
    out = pl.pallas_call(
        store_kernel,
        out_shape=jax.ShapeDtypeStruct((levels, ROWS, LANES), f32),
        in_specs=[vmem, vmem],
        out_specs=hbm,
        scratch_shapes=[pltpu.VMEM((2, ROWS, LANES), f32), dma((2 * NFLD,))],
        compiler_params=pltpu.CompilerParams(vmem_limit_bytes=2 * 1024 * 1024),
        name="store",
    )(fields, forcing)
    return out.reshape(1, NFLD, LEV, ROWS * LANES)


def solution(mesh):
    return jax.shard_map(
        functools.partial(per_device, mesh.shape["cells"]),
        mesh=mesh,
        in_specs=(
            P("group", None, None, "cells"),
            P("group", None, "cells"),
            P("group", None, "cells"),
            P("group", None, "cells"),
            P("cells"),
            P("group", None, "cells", None),
            P("group", "cells", None),
            P("group", "cells", None),
        ),
        out_specs=P("group", None, None, "cells"),
        check_vma=False,
    )
```

```python
import functools

import jax
import jax.numpy as jnp
from jax import lax
from jax.experimental import pallas as pl
from jax.experimental.pallas import tpu as pltpu
from jax.sharding import PartitionSpec as P

LANES = 128
LEV = 90
NFLD = 3
ROWS = 32
TOP = 8
RIM = 2
BATCH = 90
SLAB = 12
SLAB_STEP = 10
STRIPS = 3
MESH = pl.DeviceIdType.MESH


def lane_gather(values, index):
    return jnp.take_along_axis(values, index, axis=1, mode="promise_in_bounds")


def window_pair(rows, shift, lane):
    turned = [pltpu.roll(row, lax.rem(LANES - shift, LANES), 1) for row in rows]
    inside = lane < LANES - shift
    return [jnp.where(inside, turned[i], turned[i + 1]) for i in range(2)]


def placed(parts, first_row, shift, lane, row_of):
    turned = [pltpu.roll(part, shift, 1) for part in parts]
    late = lane >= shift
    zero = jnp.zeros_like(turned[0])
    pieces = [
        jnp.where(late, turned[0], zero),
        jnp.where(late, turned[1], turned[0]),
        jnp.where(late, zero, turned[1]),
    ]
    total = jnp.zeros(row_of.shape, jnp.float32)
    for step, piece in enumerate(pieces):
        total = jnp.where(row_of == first_row + step, piece, total)
    return total


def window_kernel(
    n_cells,
    state,
    mixing_hbm,
    weight_hbm,
    place_hbm,
    sea_hbm,
    remap_hbm,
    offsets_hbm,
    live_hbm,
    out,
    flux,
    weight,
    place,
    sea_int,
    remap,
    offsets,
    live,
    first,
    second,
    rims,
    mixing,
    sea_out,
    sea_in,
    near_air,
    term_out,
    term_in,
    load_sem,
    halo_send,
    halo_recv,
    sea_send,
    sea_recv,
    term_send,
    term_recv,
):
    cell = lax.axis_index("cells")
    group = lax.axis_index("group")
    right = lax.rem(cell + 1, n_cells)
    left = lax.rem(cell + n_cells - 1, n_cells)
    is_ocean = group == STRIPS

    def levels_of(field):
        return pl.ds(field * LEV, LEV)

    def load_of(field):
        return pltpu.make_async_copy(
            state.at[levels_of(field)],
            first.at[levels_of(field), pl.ds(TOP, ROWS), :],
            load_sem.at[field],
        )

    top_rows = [(state.at[field * LEV], near_air.at[field, pl.ds(0, ROWS), :]) for field in range(2)]
    pairs = top_rows + [
        (sea_hbm, sea_int),
        (place_hbm, place),
        (weight_hbm, weight),
        (mixing_hbm, mixing),
        (remap_hbm, remap),
        (offsets_hbm, offsets),
        (live_hbm, live),
    ]
    others = [pltpu.make_async_copy(*pair, load_sem.at[NFLD + i]) for i, pair in enumerate(pairs)]
    for copy in others[:6]:
        copy.start()
    for field in range(NFLD):
        load_of(field).start()
    for copy in others[6:]:
        copy.start()

    barrier = pltpu.get_barrier_semaphore()
    for device in (left, right):
        pl.semaphore_signal(barrier, inc=1, device_id=(group, device), device_id_type=MESH)

    @pl.when(is_ocean)
    def _():
        for strip in range(STRIPS):
            for device in (cell, right):
                pl.semaphore_signal(barrier, inc=1, device_id=(strip, device), device_id_type=MESH)

    @pl.when(jnp.logical_not(is_ocean))
    def _():
        for device in (cell, left):
            pl.semaphore_signal(barrier, inc=1, device_id=(STRIPS, device), device_id_type=MESH)

    def halo(step, field, side):
        levels = levels_of(field)
        source, low = ((state, 0), (second, TOP))[step]
        if side == 0:
            begin, land, device = low + ROWS - RIM, TOP - RIM, right
        else:
            begin, land, device = low, 0, left
        return pltpu.make_async_remote_copy(
            src_ref=source.at[levels, pl.ds(begin, RIM), :],
            dst_ref=rims.at[step, levels, pl.ds(land, RIM), :],
            send_sem=halo_send.at[step, side, field],
            recv_sem=halo_recv.at[step, side, field],
            device_id=(group, device),
            device_id_type=MESH,
        )

    def sea_copy(strip, pair):
        return pltpu.make_async_remote_copy(
            src_ref=sea_out.at[:, pl.ds(strip * SLAB_STEP, SLAB), :],
            dst_ref=sea_in.at[pair, :, pl.ds(0, SLAB), :],
            send_sem=sea_send.at[strip, pair],
            recv_sem=sea_recv.at[pair],
            device_id=(strip, (cell, right)[pair]),
            device_id_type=MESH,
        )

    def term_copy(strip, pair):
        return pltpu.make_async_remote_copy(
            src_ref=term_out.at[pair, :, pl.ds(0, SLAB), :],
            dst_ref=term_in.at[strip, pair, :, pl.ds(0, SLAB), :],
            send_sem=term_send.at[pair],
            recv_sem=term_recv.at[strip, pair],
            device_id=(STRIPS, (cell, left)[pair]),
            device_id_type=MESH,
        )

    for copy in others[:3]:
        copy.wait()
    sea_mask = sea_int[...].astype(jnp.float32)

    @pl.when(is_ocean)
    def _():
        for field in range(2):
            sea_out[field] = near_air[field, 0:ROWS, :] * sea_mask
        sea_out[2] = sea_mask
        pl.semaphore_wait(barrier, 2 + 2 * STRIPS)
        for strip in range(STRIPS):
            for pair in range(1):
                sea_copy(strip, pair).start()

    @pl.when(jnp.logical_not(is_ocean))
    def _():
        pl.semaphore_wait(barrier, 4)

    for field in range(NFLD):
        for side in range(2):
            halo(0, field, side).start()
    @pl.when(is_ocean)
    def _():
        for strip in range(STRIPS):
            for pair in range(1, 2):
                sea_copy(strip, pair).start()
    for copy in others[3:6]:
        copy.wait()

    lane8 = lax.broadcasted_iota(jnp.int32, (8, LANES), 1)
    row8 = lax.broadcasted_iota(jnp.int32, (8, LANES), 0)
    half = lane8 < LANES // 2

    upper = row8 < 4

    def advance(source, target, target_top, field, chunks):
        def take(load):
            values = [load(8 * chunk) for chunk in chunks]
            return values[0] if len(values) == 1 else jnp.where(upper, *values)

        own_row = take(lambda row: row8 + (row + RIM))
        position = [take(lambda row: place[k, row : row + 8, :]) for k in range(3)]
        index = [p & (LANES - 1) for p in position]
        apart = [(p >> 7) - own_row for p in position]
        part = [take(lambda row: weight[k, row : row + 8, :]) for k in range(3)]
        centre = part[0] + part[1] + part[2]
        scale = jnp.where(is_ocean, take(lambda row: sea_int[row : row + 8, :]).astype(jnp.float32), 1.0)
        far_at = [apart[2] == g for g in (-2, -1, 1, 2)]
        here = [apart[k] == 0 for k in range(2)]
        steps = LEV // BATCH

        def batch(t, carry):
            begin, below = carry
            level = t * BATCH
            at = field * LEV + level

            def rows_at(b, shift):
                return take(lambda row: source[at + b, pl.ds(TOP + row + shift, 8), :])

            x = [begin] + [rows_at(b, 0) for b in range(1, BATCH)]
            x.append(rows_at(jnp.minimum(BATCH, LEV - 1 - level), 0))
            before = [rows_at(b, -1) for b in range(BATCH)]
            after = [rows_at(b, 1) for b in range(BATCH)]
            mixed = []
            for b in range(BATCH):
                before2 = rows_at(b, -2)
                after2 = rows_at(b, 2)
                value = lane_gather(x[b], index[2])
                for chosen, row in zip(far_at, (before2, before[b], after[b], after2)):
                    value = jnp.where(chosen, lane_gather(row, index[2]), value)
                mixed.append(part[2] * value - centre * x[b])
            edge = [jnp.where(half, after[b], before[b]) for b in range(BATCH)]
            for k in range(2):
                for b in range(BATCH):
                    value = jnp.where(here[k], lane_gather(x[b], index[k]), lane_gather(edge[b], index[k]))
                    mixed[b] = mixed[b] + part[k] * value
            for b in range(BATCH):
                upward = take(lambda row: mixing[level + b, row : row + 8, :]) * (x[b + 1] - x[b])
                if b == BATCH - 1:
                    upward = jnp.where(t == steps - 1, 0.0, upward)
                result = x[b] + scale * (mixed[b] + (upward - below))
                for i, chunk in enumerate(chunks):
                    low, high = (0, 8) if len(chunks) == 1 else (4 * i, 4 * i + 4)
                    row = target_top + 8 * chunk
                    target[at + b, row + low : row + high, :] = result[low:high]
                below = upward
            return x[BATCH], below

        start = take(lambda row: source[field * LEV, pl.ds(TOP + row, 8), :])
        lax.fori_loop(0, steps, batch, (start, jnp.zeros((8, LANES), jnp.float32)))

    last = ROWS // 8 - 1

    def inner(source, target, target_top, field):
        for chunks in ((1,), (2,), (last, 0)):
            advance(source, target, target_top, field, chunks)

    def outer(step, source, target, target_top, field):
        for side in range(2):
            halo(step, field, side).wait_recv()

        def land(i, c):
            for b in range(10):
                at = field * LEV + i * 10 + b
                source[at, TOP - RIM : TOP, :] = rims[step, at, TOP - RIM : TOP, :]
                source[at, TOP + ROWS : TOP + ROWS + RIM, :] = rims[step, at, 0:RIM, :]
            return c

        lax.fori_loop(0, LEV // 10, land, 0)
        advance(source, target, target_top, field, (0, last))

    lane1 = lax.broadcasted_iota(jnp.int32, (1, LANES), 1)
    lane3 = lax.broadcasted_iota(jnp.int32, (3, LANES), 1)
    lane2 = lax.broadcasted_iota(jnp.int32, (2, LANES), 1)
    row_of = lax.broadcasted_iota(jnp.int32, (ROWS, LANES), 0)
    slab_row = lax.broadcasted_iota(jnp.int32, (16, LANES), 0)

    def couple():
        gap = [jnp.zeros((ROWS, LANES), jnp.float32) for _ in range(2)]
        for field in range(2):
            near_air[field, ROWS:, :] = jnp.zeros((8, LANES), jnp.float32)
        for pair in range(2):
            sea_copy(0, pair).wait_recv()
        for pair in range(2):
            col = offsets[2 * pair]
            row = offsets[2 * pair + 1] - group * (SLAB_STEP * LANES)
            rows_live = live[pair]
            sea = window_pair(
                [sea_in[pair, :, jnp.clip((row >> 7) + i, 0, 15), :] for i in range(3)],
                row & (LANES - 1),
                lane3,
            )
            sea = [jnp.where(lane3 + i * LANES < rows_live, sea[i], 0.0) for i in range(2)]
            moved = jnp.dot(
                jnp.concatenate(sea, axis=1),
                remap[pair],
                precision=lax.Precision.HIGHEST,
                preferred_element_type=jnp.float32,
            )
            for field in range(2):
                air = window_pair(
                    [near_air[field, pl.ds(jnp.clip((col >> 7) + i, 0, ROWS), 1), :] for i in range(3)],
                    col & (LANES - 1),
                    lane1,
                )
                parts = [
                    moved[field : field + 1, i * LANES : (i + 1) * LANES]
                    - air[i] * moved[2:3, i * LANES : (i + 1) * LANES]
                    for i in range(2)
                ]
                gap[field] = gap[field] + placed(parts, col >> 7, col & (LANES - 1), lane1, row_of)
        for field in range(2):
            flux[field, 0:ROWS, :] = 0.5 * gap[field]
            flux[field, ROWS:, :] = jnp.zeros((8, LANES), jnp.float32)
        for pair in range(2):
            col = offsets[2 * pair]
            row = offsets[2 * pair + 1] - group * (SLAB_STEP * LANES)
            rows_live = live[pair]
            back = window_pair(
                [flux[:, jnp.clip((col >> 7) + i, 0, ROWS), :] for i in range(3)], col & (LANES - 1), lane2
            )
            term = lax.dot_general(
                jnp.concatenate(back, axis=1),
                remap[pair],
                (((1,), (1,)), ((), ())),
                precision=lax.Precision.HIGHEST,
                preferred_element_type=jnp.float32,
            )
            parts = [
                jnp.where(lane2 + i * LANES < rows_live, term[:, i * LANES : (i + 1) * LANES], 0.0)
                for i in range(2)
            ]
            for field in range(2):
                laid = placed(
                    [part[field : field + 1] for part in parts], row >> 7, row & (LANES - 1), lane1, slab_row
                )
                term_out[pair, field] = laid
        for strip in range(STRIPS):

            @pl.when(group == strip)
            def _():
                for pair in range(2):
                    term_copy(strip, pair).start()

    def first_section(turn, c):
        @pl.when(turn < NFLD)
        def _():
            load_of(turn).wait()
            inner(first, second, TOP, turn)

        @pl.when(turn >= 1)
        def _():
            field = turn - 1
            outer(0, first, second, TOP, field)
            for side in range(2):
                halo(1, field, side).start()

        return c

    lax.fori_loop(0, NFLD + 1, first_section, 0)
    for copy in others[6:]:
        copy.wait()

    def inner_second(field, c):
        for order, chunks in enumerate(((1,), (2,), (last, 0))):
            advance(second, out, 0, field, chunks)
            if order == 0:

                @pl.when(jnp.logical_not(is_ocean) & (field == 2))
                def _():
                    couple()

        return c

    lax.fori_loop(0, NFLD, inner_second, 0)

    def outer_second(field, c):
        outer(1, second, out, 0, field)
        return c

    lax.fori_loop(0, NFLD, outer_second, 0)

    @pl.when(is_ocean)
    def _():
        for field in range(2):
            flux[field] = jnp.zeros((ROWS + 8, LANES), jnp.float32)
        for strip in range(STRIPS):
            for pair in range(2):
                term_copy(strip, pair).wait_recv()
                for field in range(2):
                    at = slice(strip * SLAB_STEP, strip * SLAB_STEP + SLAB)
                    flux[field, at, :] = flux[field, at, :] + term_in[strip, pair, field, 0:SLAB, :]
        for field in range(2):
            flux[field, 0:ROWS, :] = -flux[field, 0:ROWS, :] * sea_mask

    for step in range(2):
        for field in range(NFLD):
            for side in range(2):
                halo(step, field, side).wait_send()

    @pl.when(is_ocean)
    def _():
        for strip in range(STRIPS):
            for pair in range(2):
                sea_copy(strip, pair).wait_send()

    @pl.when(jnp.logical_not(is_ocean))
    def _():
        for pair in range(2):
            term_copy(0, pair).wait_send()


def store_kernel(fields, forcing, out, top, sem):
    copies = []
    for field in range(NFLD):
        first = field * LEV + (1 if field < 2 else 0)
        rows = pl.ds(first, (field + 1) * LEV - first)
        copies.append(pltpu.make_async_copy(fields.at[rows], out.at[rows], sem.at[field]))
    for copy in copies:
        copy.start()
    for field in range(2):
        top[field] = fields[field * LEV] + forcing[field, 0:ROWS, :]
        copy = pltpu.make_async_copy(top.at[field], out.at[field * LEV], sem.at[NFLD + field])
        copy.start()
        copies.append(copy)
    for copy in copies:
        copy.wait()


def per_device(
    n_cells,
    state,
    vertical_mix,
    neighbour_weight,
    neighbours,
    land_sea,
    remap_weight,
    pair_offsets,
    pair_rows,
):
    hbm = pl.BlockSpec(memory_space=pltpu.HBM)
    vmem = pl.BlockSpec(memory_space=pltpu.VMEM)
    levels = NFLD * LEV
    f32 = jnp.float32
    dma = pltpu.SemaphoreType.DMA
    operands = (
        state.reshape(levels, ROWS, LANES),
        vertical_mix.reshape(LEV, ROWS, LANES),
        neighbour_weight.reshape(3, ROWS, LANES),
        neighbours.reshape(3, ROWS, LANES),
        land_sea.reshape(ROWS, LANES),
        remap_weight[0],
        pair_offsets.reshape(4),
        pair_rows.reshape(2),
    )
    fields, forcing = pl.pallas_call(
        functools.partial(window_kernel, n_cells),
        out_shape=(pltpu.VMEM((levels, ROWS, LANES), f32), pltpu.VMEM((2, ROWS + 8, LANES), f32)),
        in_specs=[hbm] * 8,
        out_specs=(vmem, vmem),
        scratch_shapes=[
            pltpu.VMEM((3, ROWS, LANES), f32),
            pltpu.VMEM((3, ROWS, LANES), jnp.int32),
            pltpu.VMEM((ROWS, LANES), jnp.int32),
            pltpu.VMEM((2, 2 * LANES, 2 * LANES), f32),
            pltpu.SMEM((4,), jnp.int32),
            pltpu.SMEM((2,), jnp.int32),
            pltpu.VMEM((levels + 2, 48, LANES), f32),
            pltpu.VMEM((levels + 2, 48, LANES), f32),
            pltpu.VMEM((2, levels, 8, LANES), f32),
            pltpu.VMEM((LEV, ROWS, LANES), f32),
            pltpu.VMEM((3, ROWS, LANES), f32),
            pltpu.VMEM((2, 3, 16, LANES), f32),
            pltpu.VMEM((2, ROWS + 8, LANES), f32),
            pltpu.VMEM((2, 2, 16, LANES), f32),
            pltpu.VMEM((STRIPS, 2, 2, 16, LANES), f32),
            dma((NFLD + 9,)),
            dma((2, 2, NFLD)),
            dma((2, 2, NFLD)),
            dma((STRIPS, 2)),
            dma((2,)),
            dma((2,)),
            dma((STRIPS, 2)),
        ],
        compiler_params=pltpu.CompilerParams(
            collective_id=0, has_side_effects=True, vmem_limit_bytes=40 * 1024 * 1024
        ),
        name="window",
    )(*(pltpu.with_memory_space_constraint(operand, pltpu.HBM) for operand in operands))
    out = pl.pallas_call(
        store_kernel,
        out_shape=jax.ShapeDtypeStruct((levels, ROWS, LANES), f32),
        in_specs=[vmem, vmem],
        out_specs=hbm,
        scratch_shapes=[pltpu.VMEM((2, ROWS, LANES), f32), dma((2 * NFLD,))],
        compiler_params=pltpu.CompilerParams(vmem_limit_bytes=2 * 1024 * 1024),
        name="store",
    )(fields, forcing)
    return out.reshape(1, NFLD, LEV, ROWS * LANES)


def solution(mesh):
    return jax.shard_map(
        functools.partial(per_device, mesh.shape["cells"]),
        mesh=mesh,
        in_specs=(
            P("group", None, None, "cells"),
            P("group", None, "cells"),
            P("group", None, "cells"),
            P("group", None, "cells"),
            P("cells"),
            P("group", None, "cells", None),
            P("group", "cells", None),
            P("group", "cells", None),
        ),
        out_specs=P("group", None, None, "cells"),
        check_vma=False,
    )
```
